128 devices in a mesh: dp: 16 (over z, x_lo, core), ctx: 8 (over x_hi, y).
Axes of the slice: x: 4 (x_hi: 2, x_lo: 2; x = x_hi * 2 + x_lo), y: 4, z: 4, core: 2. Of those that a mesh axis runs over, the one named last changes fastest.
Arguments:
- inputs: bfloat16 [16, 1024, 1024], P('dp', 'ctx'), may hold values from -6 to 6
- segments: int32 [16, 1024], P('dp', 'ctx'), may hold values from 0 to 7, as said below
- cotangent: bfloat16 [16, 1024, 1024], P('dp', 'ctx'), may hold values from -6 to 6
- qkv_weight: float32 [1024, 3072], P(('dp', 'ctx')), may hold values from -0.1875 to 0.1875
- out_weight: float32 [1024, 1024], P(('dp', 'ctx')), may hold values from -0.75 to 0.75
- up_weight: float32 [1024, 4096], P(('dp', 'ctx')), may hold values from -0.1875 to 0.1875
- down_weight: float32 [1024, 4096], P(('dp', 'ctx')), may hold values from -0.09375 to 0.09375
- vectors: float32 [13312], P(('dp', 'ctx')), may hold values from -1 to 1.5
- qkv_first: float32 [1024, 3072], P(('dp', 'ctx'))
- qkv_second: float32 [1024, 3072], P(('dp', 'ctx')), as said below
- out_first: float32 [1024, 1024], P(('dp', 'ctx'))
- out_second: float32 [1024, 1024], P(('dp', 'ctx')), as said below
- up_first: float32 [1024, 4096], P(('dp', 'ctx'))
- up_second: float32 [1024, 4096], P(('dp', 'ctx')), as said below
- down_first: float32 [1024, 4096], P(('dp', 'ctx'))
- down_second: float32 [1024, 4096], P(('dp', 'ctx')), as said below
- vec_first: float32 [13312], P(('dp', 'ctx'))
- vec_second: float32 [13312], P(('dp', 'ctx')), as said below
Outputs:
- outputs: bfloat16 [16, 1024, 1024], P('dp', 'ctx')
- input_grad: float32 [16, 1024, 1024], P('dp', 'ctx')
- qkv_new: float32 [1024, 3072], P(('dp', 'ctx'))
- qkv_first_new: float32 [1024, 3072], P(('dp', 'ctx'))
- qkv_second_new: float32 [1024, 3072], P(('dp', 'ctx'))
- out_new: float32 [1024, 1024], P(('dp', 'ctx'))
- out_first_new: float32 [1024, 1024], P(('dp', 'ctx'))
- out_second_new: float32 [1024, 1024], P(('dp', 'ctx'))
- up_new: float32 [1024, 4096], P(('dp', 'ctx'))
- up_first_new: float32 [1024, 4096], P(('dp', 'ctx'))
- up_second_new: float32 [1024, 4096], P(('dp', 'ctx'))
- down_new: float32 [1024, 4096], P(('dp', 'ctx'))
- down_first_new: float32 [1024, 4096], P(('dp', 'ctx'))
- down_second_new: float32 [1024, 4096], P(('dp', 'ctx'))
- vec_new: float32 [13312], P(('dp', 'ctx'))
- vec_first_new: float32 [13312], P(('dp', 'ctx'))
- vec_second_new: float32 [13312], P(('dp', 'ctx'))
The draws below stay inside these ranges and needn't reach their ends.
Inputs may be any that keep to these rules, and one draw needn't show every extreme that they name: `segments`: along each sequence the numbers start at 0 and never fall, rising by at most 1 from one token to the next; in every draw one sequence is a single document and another holds eight documents. `qkv_second`: positive. `out_second`: positive. `up_second`: positive. `down_second`: positive. `vec_second`: positive.
All inputs are finite; a program needn't handle non-finite values.
Results may differ from the reference program's by a relative error of at most 0.02.
Values may be sent and summed in bfloat16 or wider, within the bound.
No kernel may reach another device: no remote copies, remote signals or barrier semaphores. Data moves between devices by JAX's collectives and lax.ppermute only.
A program may use at most 192 MiB of HBM per device.

```python
import math
import jax
import jax.numpy as jnp
from jax import lax

D = 1024
H = 16
FF = 4096
HD = 64
ROT = 16
VEC = 13312
SEQ = 1024
SEQS = 16
STEP = 10


def gradient_size(factor):
    return factor * math.sqrt(SEQS * SEQ)


def first_moment(key, shape, factor):
    return jax.random.normal(key, shape, jnp.float32) * (0.1 / 0.9) * factor


def second_moment(key, shape, factor):
    spread = jnp.exp(jax.random.uniform(key, shape, jnp.float32, 0.0, math.log(4.0)))
    return spread * (0.05 / 0.95) * factor * factor


def vector_factors():
    pieces = [jnp.full((2 * D,), 0.7, jnp.float32), jnp.full((2 * D,), 0.6, jnp.float32), jnp.full((3 * D,), 0.4, jnp.float32), jnp.full((D,), 1.0, jnp.float32), jnp.full((FF,), 0.3, jnp.float32), jnp.full((D,), 1.0, jnp.float32)]
    return jnp.concatenate(pieces) * gradient_size(1.0)


def draw_segments(key, part):
    key = jax.random.fold_in(key, 11)
    key_flags, key_whole, key_busy = jax.random.split(key, 3)
    spacing = max(SEQ // 4, 2)
    flags = (jax.random.randint(key_flags, (SEQS, SEQ), 0, spacing) == 0).astype(jnp.int32)
    flags = flags.at[:, 0].set(0)
    whole = jax.random.randint(key_whole, (), 0, SEQS)
    busy = (whole + 1) % SEQS
    picks = jax.random.permutation(key_busy, SEQ - 1)[:7] + 1
    busy_flags = jnp.zeros((SEQ,), jnp.int32).at[picks].set(1)
    row_ids = jnp.arange(SEQS, dtype=jnp.int32)[:, None]
    flags = jnp.where(row_ids == busy, busy_flags[None, :], flags)
    flags = jnp.where(row_ids == whole, 0, flags)
    return jnp.minimum(jnp.cumsum(flags, axis=1), 7).astype(jnp.int32)


def draw_vectors(key, part):
    key = jax.random.fold_in(key, 21)
    key_gain, key_shift = jax.random.split(key)
    gains = jax.random.uniform(key_gain, (2, D), jnp.float32, 0.5, 1.5)
    shifts = jnp.clip(0.2 * jax.random.normal(key_shift, (VEC,), jnp.float32), -1.0, 1.0)
    shifts = shifts.at[0:D].set(gains[0])
    shifts = shifts.at[2 * D:3 * D].set(gains[1])
    return shifts


def draw_qkv_first(key, part):
    key = jax.random.fold_in(key, 31)
    return first_moment(key, (D, 3 * D), gradient_size(0.4))


def draw_qkv_second(key, part):
    key = jax.random.fold_in(key, 32)
    return second_moment(key, (D, 3 * D), gradient_size(0.4))


def draw_out_first(key, part):
    key = jax.random.fold_in(key, 41)
    return first_moment(key, (D, D), gradient_size(0.15))


def draw_out_second(key, part):
    key = jax.random.fold_in(key, 42)
    return second_moment(key, (D, D), gradient_size(0.15))


def draw_up_first(key, part):
    key = jax.random.fold_in(key, 51)
    return first_moment(key, (D, FF), gradient_size(0.3))


def draw_up_second(key, part):
    key = jax.random.fold_in(key, 52)
    return second_moment(key, (D, FF), gradient_size(0.3))


def draw_down_first(key, part):
    key = jax.random.fold_in(key, 61)
    return first_moment(key, (D, FF), gradient_size(0.65))


def draw_down_second(key, part):
    key = jax.random.fold_in(key, 62)
    return second_moment(key, (D, FF), gradient_size(0.65))


def draw_vec_first(key, part):
    key = jax.random.fold_in(key, 71)
    return first_moment(key, (VEC,), vector_factors())


def draw_vec_second(key, part):
    key = jax.random.fold_in(key, 72)
    return second_moment(key, (VEC,), vector_factors())


def block_scale(key, dims, cuts, least, largest):
    def one(position, parts):
        heights = jax.random.uniform(jax.random.fold_in(jax.random.fold_in(key, 6), position), (parts,), jnp.float32, least / len(cuts), largest / len(cuts))
        return jnp.repeat(jnp.exp(heights), dims[position] // parts).reshape((-1,) + (1,) * (len(dims) - position - 1))

    loudness = one(*cuts[0])
    for cut in cuts[1:]:
        loudness = loudness * one(*cut)
    return loudness


def gaussian(stream_key, extent, scale, most, cuts=(), kind=jnp.bfloat16):
    values = scale * jax.random.normal(stream_key, extent, jnp.float32)
    if cuts:
        values = values * block_scale(stream_key, extent, cuts, -0.22, 0.18)
    return jnp.clip(values, -most, most).astype(kind)


def setup_inputs(seed: int = 0) -> dict:
    streams_of = jax.random.split(jax.random.key(seed), 19)
    inputs = gaussian(streams_of[0], (SEQS, SEQ, D), 1.0, 6.0, ((0, 16), (1, 8)))
    segments = draw_segments(jax.random.fold_in(streams_of[18], 71), 0)
    cotangent = gaussian(streams_of[2], (SEQS, SEQ, D), 1.0, 6.0, ((0, 16), (1, 8)))
    qkv_weight = gaussian(streams_of[3], (D, 3 * D), D ** -0.5, 0.1875, ((0, 128),), jnp.float32)
    out_weight = gaussian(streams_of[4], (D, D), (D // 16) ** -0.5, 0.75, ((0, 128),), jnp.float32)
    up_weight = gaussian(streams_of[5], (D, FF), D ** -0.5, 0.1875, ((0, 128),), jnp.float32)
    down_weight = gaussian(streams_of[6], (D, FF), FF ** -0.5, 0.09375, ((0, 128),), jnp.float32)
    vectors = draw_vectors(jax.random.fold_in(streams_of[18], 71), 0)
    qkv_first = draw_qkv_first(jax.random.fold_in(streams_of[18], 71), 0)
    qkv_second = draw_qkv_second(jax.random.fold_in(streams_of[18], 71), 0)
    out_first = draw_out_first(jax.random.fold_in(streams_of[18], 71), 0)
    out_second = draw_out_second(jax.random.fold_in(streams_of[18], 71), 0)
    up_first = draw_up_first(jax.random.fold_in(streams_of[18], 71), 0)
    up_second = draw_up_second(jax.random.fold_in(streams_of[18], 71), 0)
    down_first = draw_down_first(jax.random.fold_in(streams_of[18], 71), 0)
    down_second = draw_down_second(jax.random.fold_in(streams_of[18], 71), 0)
    vec_first = draw_vec_first(jax.random.fold_in(streams_of[18], 71), 0)
    vec_second = draw_vec_second(jax.random.fold_in(streams_of[18], 71), 0)
    return {"inputs": inputs, "segments": segments, "cotangent": cotangent, "qkv_weight": qkv_weight, "out_weight": out_weight, "up_weight": up_weight, "down_weight": down_weight, "vectors": vectors, "qkv_first": qkv_first, "qkv_second": qkv_second, "out_first": out_first, "out_second": out_second, "up_first": up_first, "up_second": up_second, "down_first": down_first, "down_second": down_second, "vec_first": vec_first, "vec_second": vec_second}


@jax.custom_vjp
def low(v):
    return lax.optimization_barrier(v.astype(jnp.bfloat16)).astype(jnp.float32)

@jax.custom_vjp
def low_back(v):
    return v

def low_keep(v):
    return (low(v), None)

def low_pass(kept, grad):
    return (grad,)

def back_keep(v):
    return (v, None)

def back_low(kept, grad):
    return (low(grad),)
low.defvjp(low_keep, low_pass)
low_back.defvjp(back_keep, back_low)
highest = lax.Precision.HIGHEST
beta_one = 0.9
beta_two = 0.95
epsilon = 1e-08
norm_epsilon = 1e-05

def matmul(left, right):
    return jnp.dot(left, right, precision=highest, preferred_element_type=jnp.float32)

def split_vectors(vectors):
    sizes_list = [D, D, D, D, 3 * D, D, FF, D]
    pieces = []
    offset_now = 0
    for width in sizes_list:
        pieces.append(vectors[offset_now:offset_now + width])
        offset_now = offset_now + width
    return pieces

def layer_norm(values, norm_gain, norm_shift):
    center = values - lax.optimization_barrier(jnp.mean(values, axis=-1, keepdims=True))
    spread = lax.optimization_barrier(jnp.mean(center * center, axis=-1, keepdims=True))
    return center * lax.rsqrt(spread + norm_epsilon) * norm_gain + norm_shift

def rotate(values, positions):
    half_width = ROT // 2
    frequency = 10000.0 ** (-jnp.arange(half_width, dtype=jnp.float32) * 2.0 / ROT)
    angles = positions.astype(jnp.float32)[:, None] * frequency[None, :]
    cosine = jnp.concatenate([jnp.cos(angles), jnp.cos(angles)], axis=-1)[:, None, :]
    sines = jnp.concatenate([jnp.sin(angles), jnp.sin(angles)], axis=-1)[:, None, :]
    rotated = values[..., :ROT]
    lower_half = rotated[..., :half_width]
    upper_half = rotated[..., half_width:]
    turned = jnp.concatenate([-upper_half, lower_half], axis=-1)
    return jnp.concatenate([rotated * cosine + turned * sines, values[..., ROT:]], axis=-1)

def doc_starts(doc_marks):
    token_index = jnp.arange(SEQ, dtype=jnp.int32)
    boundary = jnp.concatenate([jnp.ones((1,), bool), doc_marks[1:] != doc_marks[:-1]])
    return lax.cummax(jnp.where(boundary, token_index, 0).astype(jnp.int32), axis=0)

def forward(tokens, starts, qkv_weight, out_weight, up_weight, down_weight, vectors):
    qkv_weight = low(qkv_weight)
    out_weight = low(out_weight)
    up_weight = low(up_weight)
    down_weight = low(down_weight)
    vectors = low(vectors)
    gain_one, shift_one, gain_two, shift_two, bias_qkv, bias_out, bias_up, bias_down = split_vectors(vectors)
    normed_one = low(layer_norm(tokens, gain_one, shift_one))
    normed_two = low(layer_norm(tokens, gain_two, shift_two))
    projected = low_back(matmul(normed_one, qkv_weight) + bias_qkv).reshape(SEQ, H, 3, HD)
    token_index = jnp.arange(SEQ, dtype=jnp.int32)
    positions = token_index - starts
    queries = low(rotate(projected[:, :, 0], positions))
    keys_all = low(rotate(projected[:, :, 1], positions))
    values_all = low(projected[:, :, 2])
    block_rows = min(SEQ, 512)

    def attend(pieces):
        query_rows, row_index, row_start = pieces
        products = jnp.einsum('qhd,khd->hqk', query_rows, keys_all, precision=highest) / math.sqrt(HD)
        scores = low_back(products)
        allowed = (token_index[None, :] <= row_index[:, None]) & (token_index[None, :] >= row_start[:, None])
        scores = jnp.where(allowed[None], scores, -jnp.inf)
        row_max = lax.optimization_barrier(jnp.max(scores, axis=-1, keepdims=True))
        expo = jnp.exp(scores - row_max)
        weights = low(expo / lax.optimization_barrier(jnp.sum(expo, axis=-1, keepdims=True)))
        return jnp.einsum('hqk,khd->qhd', weights, values_all, precision=highest)
    blocks = SEQ // block_rows
    attended = lax.map(jax.checkpoint(attend), (queries.reshape(blocks, block_rows, H, HD), token_index.reshape(blocks, block_rows), starts.reshape(blocks, block_rows)))
    attended = low(low_back(attended.reshape(SEQ, D)))
    attention = matmul(attended, out_weight.T) + bias_out
    hidden = low_back(matmul(normed_two, up_weight) + bias_up)
    active = low(jax.nn.gelu(hidden, approximate=False))
    feed = matmul(active, down_weight.T) + bias_down
    return tokens + attention + feed

def adamw(weight, moment_one, moment_two, gradient, step_rate, decay_rate):
    moment_one = beta_one * moment_one + (1.0 - beta_one) * gradient
    moment_two = beta_two * moment_two + (1.0 - beta_two) * gradient * gradient
    fix_one = 1.0 - beta_one ** STEP
    fix_two = 1.0 - beta_two ** STEP
    update = moment_one / fix_one / (jnp.sqrt(moment_two / fix_two) + epsilon)
    weight = weight - step_rate * (update + decay_rate * weight)
    return (weight, moment_one, moment_two)

def step_rates():
    return (2.0 / math.sqrt(D), 8.0 / math.sqrt(D), 2.0 / math.sqrt(D), 2.0 / math.sqrt(FF), 0.5)

def reference(inputs, segments, cotangent, qkv_weight, out_weight, up_weight, down_weight, vectors, qkv_first, qkv_second, out_first, out_second, up_first, up_second, down_first, down_second, vec_first, vec_second):
    weights = (qkv_weight, out_weight, up_weight, down_weight, vectors)

    def per_sequence(totals, pieces):
        tokens, doc_marks, upstream = pieces
        tokens = tokens.astype(jnp.float32)
        starts = doc_starts(doc_marks)

        def closed(token_values, qkv_value, out_value, up_value, down_value, vector_value):
            return forward(token_values, starts, qkv_value, out_value, up_value, down_value, vector_value)
        result, pullback = jax.vjp(closed, tokens, *weights)
        gradients = pullback(upstream.astype(jnp.float32))
        totals = tuple((left_sum + right_sum for left_sum, right_sum in zip(totals, gradients[1:])))
        return (totals, (result.astype(jnp.bfloat16), gradients[0]))
    zero_sums = tuple((jnp.zeros_like(weight) for weight in weights))
    totals, (outputs, input_grad) = lax.scan(per_sequence, zero_sums, (inputs, segments, cotangent))
    moments = ((qkv_first, qkv_second), (out_first, out_second), (up_first, up_second), (down_first, down_second), (vec_first, vec_second))
    decays = (0.1, 0.1, 0.1, 0.1, 0.0)
    results = [outputs, input_grad]
    for weight, pair, gradient, step_rate, decay_rate in zip(weights, moments, totals, step_rates(), decays):
        results.extend(adamw(weight, pair[0], pair[1], gradient, step_rate, decay_rate))
    return tuple(results)
```

```python
import math

import jax
import jax.numpy as jnp
from jax import lax
from jax.experimental import pallas as pl
from jax.experimental.pallas import tpu as pltpu
from jax.sharding import PartitionSpec as P

D = 1024
H = 16
FF = 4096
HD = 64
ROT = 16
STEP = 10
SEQ = 1024
TP = 8
HEADS = H // TP
QKV = 3 * D // TP
OUT = D // TP
UP = FF // TP
EXTRA = 128
BLOCK = 256

beta_one = 0.9
beta_two = 0.95
epsilon = 1e-08
norm_epsilon = 1e-05
low = jnp.bfloat16
full = jnp.float32


def dot(a, b, dims=((1,), (0,))):
    return lax.dot_general(a, b, (dims, ((), ())), preferred_element_type=full)


NT = ((1,), (1,))
TN = ((0,), (0,))


def adamw(weight, moment_one, moment_two, gradient, step_rate, decay_rate):
    moment_one = beta_one * moment_one + (1.0 - beta_one) * gradient
    moment_two = beta_two * moment_two + (1.0 - beta_two) * gradient * gradient
    fix_one = 1.0 - beta_one**STEP
    fix_two = 1.0 - beta_two**STEP
    update = moment_one / fix_one / (jnp.sqrt(moment_two / fix_two) + epsilon)
    weight = weight - step_rate * (update + decay_rate * weight)
    return (weight, moment_one, moment_two)


def normalise(values):
    center = values - jnp.mean(values, axis=-1, keepdims=True)
    spread = jnp.mean(center * center, axis=-1, keepdims=True)
    rate = lax.rsqrt(spread + norm_epsilon)
    return center * rate, rate


def x_pairs():
    return [(i, (i + 4) % 8) for i in range(8)]


def y_pairs(step):
    return [(a * 4 + b, a * 4 + (b + step) % 4) for a in range(2) for b in range(4)]


def gather_ctx(part):
    place = lax.axis_index("ctx")
    half, row = place // 4, lax.rem(place, 4)
    rows, width = part.shape
    other = lax.ppermute(part, "ctx", x_pairs())
    pair = jnp.concatenate([part, other], axis=0)
    above = lax.ppermute(pair, "ctx", y_pairs(1))
    below = lax.ppermute(pair, "ctx", y_pairs(-1))
    far_own = lax.ppermute(above[:rows], "ctx", y_pairs(1))
    far_other = lax.ppermute(below[rows:], "ctx", y_pairs(-1))
    whole = jnp.zeros((8 * rows, width), part.dtype)
    pieces = (
        (part, half, row),
        (other, 1 - half, row),
        (above[:rows], half, row + 3),
        (above[rows:], 1 - half, row + 3),
        (below[:rows], half, row + 1),
        (below[rows:], 1 - half, row + 1),
        (far_own, half, row + 2),
        (far_other, 1 - half, row + 2),
    )
    for piece, at_half, at_row in pieces:
        spot = at_half * 4 + lax.rem(at_row, 4)
        whole = lax.dynamic_update_slice(whole, piece, (spot * rows, 0))
    return whole


def turn(values, cosine, sine):
    lane = lax.broadcasted_iota(jnp.int32, values.shape, 1) % HD
    ahead = pltpu.roll(values, values.shape[1] - ROT // 2, 1)
    behind = pltpu.roll(values, ROT // 2, 1)
    turned = jnp.where(lane < ROT // 2, -ahead, behind)
    return jnp.where(lane < ROT, values * cosine + turned * sine, values)


def attention_kernel(projected, cosine, sine, starts, d_out, out, d_projected, q_s, k_s, v_s, dq_s, dk_s, dv_s):
    width = HEADS * HD
    for block in range(SEQ // BLOCK):
        rows = pl.ds(block * BLOCK, BLOCK)
        q_s[rows, :] = (turn(projected[rows, 0:width], cosine[rows, :], sine[rows, :]).astype(low) * (HD**-0.5)).astype(low)
        k_s[rows, :] = turn(projected[rows, width : 2 * width], cosine[rows, :], sine[rows, :]).astype(low)
        v_s[rows, :] = projected[rows, 2 * width : 3 * width].astype(low)
    dk_s[...] = jnp.zeros_like(dk_s)
    dv_s[...] = jnp.zeros_like(dv_s)
    for block in range(SEQ // BLOCK):
        rows = pl.ds(block * BLOCK, BLOCK)
        keys = (block + 1) * BLOCK
        row_index = block * BLOCK + lax.broadcasted_iota(jnp.int32, (BLOCK, keys), 0)
        key_index = lax.broadcasted_iota(jnp.int32, (BLOCK, keys), 1)
        allowed = (key_index <= row_index) & (key_index >= starts[rows, :])
        for head in range(HEADS):
            lanes = pl.ds(head * HD, HD)
            q = q_s[rows, lanes]
            k = k_s[0:keys, lanes]
            v = v_s[0:keys, lanes]
            d_o = d_out[rows, lanes]
            scores = jnp.where(allowed, dot(q, k, NT), -1e30)
            expo = jnp.exp(scores - jnp.max(scores, axis=-1, keepdims=True))
            weight = expo * (1.0 / jnp.sum(expo, axis=-1, keepdims=True))
            weight_low = weight.astype(low)
            attended = dot(weight_low, v)
            out[rows, lanes] = attended.astype(low)
            delta = jnp.sum(attended * d_o.astype(full), axis=-1, keepdims=True)
            d_scores = (weight * (dot(d_o, v, NT) - delta)).astype(low)
            dq_s[rows, lanes] = dot(d_scores, k) * (HD**-0.5)
            dk_s[0:keys, lanes] += dot(d_scores, q, TN)
            dv_s[0:keys, lanes] += dot(weight_low, d_o, TN)
    for block in range(SEQ // BLOCK):
        rows = pl.ds(block * BLOCK, BLOCK)
        d_projected[rows, 0:width] = turn(dq_s[rows, :], cosine[rows, :], -sine[rows, :]).astype(low)
        d_projected[rows, width : 2 * width] = turn(dk_s[rows, :], cosine[rows, :], -sine[rows, :]).astype(low)
        d_projected[rows, 2 * width : 3 * width] = dv_s[rows, :].astype(low)


def attention(projected, cosine, sine, starts, d_out):
    width = HEADS * HD
    vmem = pl.BlockSpec(memory_space=pltpu.VMEM)
    return pl.pallas_call(
        attention_kernel,
        out_shape=(
            jax.ShapeDtypeStruct((SEQ, width), low),
            jax.ShapeDtypeStruct((SEQ, 3 * width), low),
        ),
        in_specs=[vmem] * 5,
        out_specs=(vmem, vmem),
        scratch_shapes=[pltpu.VMEM((SEQ, width), low)] * 3 + [pltpu.VMEM((SEQ, width), full)] * 3,
        compiler_params=pltpu.CompilerParams(vmem_limit_bytes=40 * 2**20),
        cost_estimate=pl.CostEstimate(
            flops=14 * HEADS * SEQ * SEQ * HD, bytes_accessed=8 * SEQ * 3 * width, transcendentals=HEADS * SEQ * SEQ
        ),
        name="attention",
    )(projected, cosine, sine, starts, d_out)


def local(
    inputs, segments, cotangent, qkv_weight, out_weight, up_weight, down_weight, vectors,
    qkv_first, qkv_second, out_first, out_second, up_first, up_second, down_first, down_second, vec_first, vec_second,
):
    place = lax.axis_index("ctx")
    tokens = inputs[0]
    upstream = cotangent[0]

    def cut(weight):
        return weight.astype(low).reshape(8, TP, -1).transpose(1, 0, 2)

    qkv_cut = qkv_weight.astype(low).reshape(8, TP, HEADS, 3, HD).transpose(1, 0, 3, 2, 4).reshape(TP, 8, QKV)
    extra = jnp.concatenate(
        [
            segments[0].astype(low).reshape(8, 16),
            vectors.astype(low).reshape(8, 13),
            jnp.zeros((8, EXTRA - 29), low),
        ],
        axis=1,
    )
    parcel = jnp.concatenate(
        [qkv_cut, cut(out_weight), cut(up_weight), cut(down_weight), jnp.broadcast_to(extra, (TP, 8, EXTRA))], axis=2
    )
    parcel = lax.all_to_all(parcel, "ctx", 0, 0, tiled=True)
    marks = parcel[:, :, QKV + OUT + 2 * UP : QKV + OUT + 2 * UP + 16].reshape(SEQ).astype(jnp.int32)
    gathered = lax.all_gather(parcel.reshape(64, -1), "dp", axis=0, tiled=True)

    counts = jnp.sum(marks[None, :] < jnp.arange(8)[:, None], axis=1)
    starts = jnp.sum(jnp.where(marks[:, None] == jnp.arange(8)[None, :], counts[None, :], 0), axis=1)
    positions = (jnp.arange(SEQ, dtype=jnp.int32) - starts).astype(full)
    frequency = 10000.0 ** (-jnp.arange(ROT // 2, dtype=full) * 2.0 / ROT)
    angles = positions[:, None] * jnp.tile(frequency, HEADS * HD // (ROT // 2))[None, :]
    cosine, sine = jnp.cos(angles), jnp.sin(angles)

    x = gather_ctx(tokens)
    dy = gather_ctx(upstream)
    normed = normalise(x.astype(full))[0].astype(low)

    w_qkv = gathered[:, 0:QKV]
    w_out = gathered[:, QKV : QKV + OUT]
    w_up = gathered[:, QKV + OUT : QKV + OUT + UP]
    w_down = gathered[:, QKV + OUT + UP : QKV + OUT + 2 * UP]
    vec = gathered[:, QKV + OUT + 2 * UP + 16 : QKV + OUT + 2 * UP + 29].reshape(-1)
    gain_one, shift_one, gain_two, shift_two = (vec[i * D : (i + 1) * D] for i in range(4))
    bias_qkv = lax.dynamic_slice(vec, (4 * D + QKV * place,), (QKV,)).reshape(HEADS, 3, HD).transpose(1, 0, 2).reshape(QKV)
    bias_up = lax.dynamic_slice(vec, (8 * D + UP * place,), (UP,))
    bias_out = vec[7 * D : 8 * D].astype(full) + vec[12 * D : 13 * D].astype(full)
    scaled_qkv = (gain_one.astype(full)[:, None] * w_qkv.astype(full)).astype(low)
    scaled_up = (gain_two.astype(full)[:, None] * w_up.astype(full)).astype(low)
    base_qkv = dot(shift_one[None], w_qkv) + bias_qkv.astype(full)
    base_up = dot(shift_two[None], w_up) + bias_up.astype(full)

    hidden = dot(normed, scaled_up) + base_up
    gate = 0.5 * (1.0 + lax.erf(hidden * (0.5**0.5)))
    active = (hidden * gate).astype(low)
    slope = gate + hidden * jnp.exp(-0.5 * hidden * hidden) * (1.0 / math.sqrt(2.0 * math.pi))
    d_hidden = (dot(dy, w_down) * slope).astype(low)
    up_core = dot(normed, d_hidden, TN)
    hidden_total = jnp.sum(d_hidden.astype(full), axis=0)
    grad_up = gain_two.astype(full)[:, None] * up_core + shift_two.astype(full)[:, None] * hidden_total[None]
    grad_down = dot(dy, active, TN)
    sent = jnp.concatenate([grad_up.astype(low), grad_down.astype(low)], axis=1)
    feed_grads = lax.all_to_all(sent.reshape(128, 8, 2 * UP), ("dp", "ctx"), 0, 0, tiled=True)

    projected = dot(normed, scaled_qkv) + base_qkv
    d_out = dot(dy, w_out).astype(low)
    attended, d_projected = attention(projected, cosine, sine, starts[:, None], d_out)
    d_x = dot(d_projected, scaled_qkv, NT) + dot(d_hidden, scaled_up, NT)
    d_x = lax.all_to_all(d_x.astype(low).reshape(TP, SEQ // TP, D), "ctx", 0, 0, tiled=True)
    result = dot(attended, w_out, NT) + dot(active, w_down, NT)
    result = lax.all_to_all(result.astype(low).reshape(TP, SEQ // TP, D), "ctx", 0, 0, tiled=True)

    qkv_core = dot(normed, d_projected, TN)
    projected_total = jnp.sum(d_projected.astype(full), axis=0)
    grad_qkv = gain_one.astype(full)[:, None] * qkv_core + shift_one.astype(full)[:, None] * projected_total[None]
    grad_out = dot(dy, attended, TN)
    grad_gain_one = jnp.sum(w_qkv.astype(full) * qkv_core, axis=1)
    grad_gain_two = jnp.sum(w_up.astype(full) * up_core, axis=1)
    grad_shift_one = jnp.sum(w_qkv.astype(full) * projected_total[None], axis=1)
    grad_shift_two = jnp.sum(w_up.astype(full) * hidden_total[None], axis=1)
    upstream_total = jnp.sum(upstream.astype(full), axis=0)
    grad_bias_qkv = projected_total.reshape(3, HEADS, HD).transpose(1, 0, 2).reshape(QKV)
    grad_vectors = jnp.concatenate(
        [
            grad_gain_one,
            grad_shift_one,
            grad_gain_two,
            grad_shift_two,
            lax.dynamic_update_slice(jnp.zeros((3 * D,), full), grad_bias_qkv, (QKV * place,)),
            upstream_total,
            lax.dynamic_update_slice(jnp.zeros((FF,), full), hidden_total, (UP * place,)),
            upstream_total,
        ]
    )
    sent = jnp.concatenate(
        [
            grad_qkv.astype(low).reshape(128, 8, QKV),
            grad_out.astype(low).reshape(128, 8, OUT),
            grad_vectors.astype(low).reshape(128, 8, 13),
            jnp.zeros((128, 8, EXTRA - 13), low),
        ],
        axis=2,
    )
    rest_grads = lax.all_to_all(sent, ("dp", "ctx"), 0, 0, tiled=True)

    outputs = tokens.astype(full) + jnp.sum(result.astype(full), axis=0) + bias_out
    own, rate = normalise(tokens.astype(full))
    d_own = jnp.sum(d_x.astype(full), axis=0)
    d_tokens = rate * (
        d_own - jnp.mean(d_own, axis=-1, keepdims=True) - own * jnp.mean(d_own * own, axis=-1, keepdims=True)
    )
    input_grad = upstream.astype(full) + d_tokens

    feed_grads = jnp.sum(feed_grads.reshape(16, TP, 8, 2 * UP).astype(full), axis=0)
    rest_grads = jnp.sum(rest_grads.reshape(16, TP, 8, QKV + OUT + EXTRA).astype(full), axis=0)
    up_grad = feed_grads[:, :, :UP].transpose(1, 0, 2).reshape(8, FF)
    down_grad = feed_grads[:, :, UP:].transpose(1, 0, 2).reshape(8, FF)
    qkv_grad = rest_grads[:, :, :QKV].reshape(TP, 8, 3, HEADS, HD).transpose(1, 0, 3, 2, 4).reshape(8, 3 * D)
    out_grad = rest_grads[:, :, QKV : QKV + OUT].transpose(1, 0, 2).reshape(8, D)
    vector_grad = jnp.sum(rest_grads[:, :, QKV + OUT : QKV + OUT + 13], axis=0).reshape(104)

    qkv_new = adamw(qkv_weight, qkv_first, qkv_second, qkv_grad, 2.0 / math.sqrt(D), 0.1)
    out_new = adamw(out_weight, out_first, out_second, out_grad, 8.0 / math.sqrt(D), 0.1)
    up_new = adamw(up_weight, up_first, up_second, up_grad, 2.0 / math.sqrt(D), 0.1)
    down_new = adamw(down_weight, down_first, down_second, down_grad, 2.0 / math.sqrt(FF), 0.1)
    vec_new = adamw(vectors, vec_first, vec_second, vector_grad, 0.5, 0.0)
    return (outputs.astype(low)[None], input_grad[None]) + qkv_new + out_new + up_new + down_new + vec_new


def solution(mesh):
    tokens = P("dp", "ctx", None)
    matrix = P(("dp", "ctx"), None)
    vector = P(("dp", "ctx"))
    return jax.shard_map(
        local,
        mesh=mesh,
        in_specs=(tokens, P("dp", "ctx"), tokens) + (matrix,) * 4 + (vector,) + (matrix,) * 8 + (vector,) * 2,
        out_specs=(tokens, tokens) + (matrix,) * 12 + (vector,) * 3,
        check_vma=False,
    )
```

```python
import math

import jax
import jax.numpy as jnp
import numpy as np
from jax import lax
from jax.experimental import pallas as pl
from jax.experimental.pallas import tpu as pltpu
from jax.sharding import PartitionSpec as P

D = 1024
H = 16
FF = 4096
HD = 64
ROT = 16
STEP = 10
SEQ = 1024
TP = 8
ROWS = SEQ // TP
HEADS = H // TP
WIDTH = HEADS * HD
QKV = 3 * D // TP
OUT = D // TP
UP = FF // TP
EXTRA = 128
MIXED = UP + QKV
FEED = 2 * UP + OUT
BLOCK = 256

beta_one = 0.9
beta_two = 0.95
epsilon = 1e-08
norm_epsilon = 1e-05
FREQUENCIES = [float(f) for f in 10000.0 ** (-np.arange(ROT // 2, dtype=np.float32) * np.float32(2.0) / np.float32(ROT))]
low = jnp.bfloat16
full = jnp.float32

AT_UP = 0
AT_QKV = UP
AT_OUT = UP + QKV
AT_DOWN = AT_OUT + OUT
AT_EXTRA = AT_DOWN + UP
PARCEL = AT_EXTRA + EXTRA

NT = ((1,), (1,))
TN = ((0,), (0,))
VMEM = pl.BlockSpec(memory_space=pltpu.VMEM)
SMEM = pl.BlockSpec(memory_space=pltpu.SMEM)


def dot(a, b, dims=((1,), (0,))):
    return lax.dot_general(a, b, (dims, ((), ())), preferred_element_type=full)


def call(kernel, name, out_shape, in_specs, operands, scratch=(), limit=56, grid=()):
    return pl.pallas_call(
        kernel,
        grid=grid,
        out_shape=tuple(jax.ShapeDtypeStruct(*s) for s in out_shape),
        in_specs=in_specs,
        out_specs=(VMEM,) * len(out_shape),
        scratch_shapes=list(scratch),
        compiler_params=pltpu.CompilerParams(vmem_limit_bytes=limit * 2**20),
        cost_estimate=pl.CostEstimate(flops=1024, bytes_accessed=1024, transcendentals=0),
        name=name,
    )(*operands)


def adamw(weight, moment_one, moment_two, gradient, step_rate, decay_rate):
    moment_one = beta_one * moment_one + (1.0 - beta_one) * gradient
    moment_two = beta_two * moment_two + (1.0 - beta_two) * gradient * gradient
    fix_one = 1.0 - beta_one**STEP
    fix_two = 1.0 - beta_two**STEP
    update = moment_one / fix_one / (jnp.sqrt(moment_two / fix_two) + epsilon)
    weight = weight - step_rate * (update + decay_rate * weight)
    return (weight, moment_one, moment_two)


def normalise(values):
    center = values - jnp.mean(values, axis=-1, keepdims=True)
    spread = jnp.mean(center * center, axis=-1, keepdims=True)
    rate = lax.rsqrt(spread + norm_epsilon)
    return center * rate, rate


def across(value):
    return lax.ppermute(value, "ctx", [(i, (i + 4) % 8) for i in range(8)])


def along(value, step):
    return lax.ppermute(value, "ctx", [(a * 4 + b, a * 4 + (b + step) % 4) for a in range(2) for b in range(4)])


def other_core(value):
    return lax.ppermute(value, "dp", [(i, i ^ 1) for i in range(16)])


def spot_of(place, far, step):
    half, row = place // 4, place % 4
    half = 1 - half if far else half
    return half * 4 + (row + step) % 4


def pack_kernel(qkv, out, up, down, vec, marks, parcel):
    extra = jnp.concatenate([vec[...], marks[...].astype(full), jnp.zeros((6, EXTRA), full)], axis=0).astype(low)
    for c in range(TP):
        for part in range(3):
            for head in range(HEADS):
                start = c * QKV + (head * 3 + part) * HD
                at = AT_QKV + part * WIDTH + head * HD
                parcel[c, :, at : at + HD] = qkv[:, start : start + HD].astype(low)
        parcel[c, :, AT_UP : AT_UP + UP] = up[:, c * UP : (c + 1) * UP].astype(low)
        parcel[c, :, AT_OUT : AT_OUT + OUT] = out[:, c * OUT : (c + 1) * OUT].astype(low)
        parcel[c, :, AT_DOWN : AT_DOWN + UP] = down[:, c * UP : (c + 1) * UP].astype(low)
        parcel[c, :, AT_EXTRA:PARCEL] = extra


def starts_kernel(marks, starts, cosine, sine):
    whole = marks[...]
    start = jnp.zeros_like(whole)
    for k in range(1, 8):
        start = jnp.where(whole == k, jnp.sum((whole < k).astype(full), keepdims=True), start)
    row = lax.broadcasted_iota(jnp.int32, whole.shape, 0) * ROWS + lax.broadcasted_iota(jnp.int32, whole.shape, 1)
    positions = row.astype(full) - start
    slow = lax.broadcasted_iota(jnp.int32, (ROT // 2, 1), 0)
    frequency = jnp.zeros((ROT // 2, 1), full)
    for i, value in enumerate(FREQUENCIES):
        frequency = jnp.where(slow == i, value, frequency)
    rest = jnp.zeros((ROWS, HD - ROT), full)
    turned = start.T
    for block in range(TP):
        rows = slice(block * ROWS, (block + 1) * ROWS)
        angles = positions[block : block + 1, :] * frequency
        cos_one = jnp.cos(angles).T
        sin_one = jnp.sin(angles).T
        cosine[rows, :] = jnp.concatenate([cos_one, cos_one, rest] * HEADS, axis=1)
        sine[rows, :] = jnp.concatenate([sin_one, sin_one, rest] * HEADS, axis=1)
        starts[rows, :] = turned[:, block : block + 1].astype(jnp.int32)


def norm_kernel(place, *refs):
    pieces, (whole, turned) = refs[:4], refs[4:]
    for step in range(4):
        for far in range(2):
            spot = pl.multiple_of(spot_of(place[0], far, step) * ROWS, ROWS)
            normed, _ = normalise(pieces[step][far * ROWS : (far + 1) * ROWS, :].astype(full))
            normed = normed.astype(low)
            whole[pl.ds(spot, ROWS), :] = normed
            turned[:, pl.ds(spot, ROWS)] = normed.T


def collect_kernel(place, *refs):
    pieces, (whole, turned) = refs[:4], refs[4:]
    for step in range(4):
        for far in range(2):
            spot = pl.multiple_of(spot_of(place[0], far, step) * ROWS, ROWS)
            piece = pieces[step][far * ROWS : (far + 1) * ROWS, :]
            whole[pl.ds(spot, ROWS), :] = piece
            turned[:, pl.ds(spot, ROWS)] = piece.T


def split_cores(core, rows):
    blocks = rows.reshape(rows.shape[0] // 128, 2, 64, rows.shape[1])
    mine = jnp.where(core == 0, blocks[:, 0], blocks[:, 1])
    others = jnp.where(core == 0, blocks[:, 1], blocks[:, 0])
    return mine.astype(low), others.astype(low)


def turn(values, cosine, sine):
    lane = lax.broadcasted_iota(jnp.int32, values.shape, 1) % HD
    ahead = pltpu.roll(values, values.shape[1] - ROT // 2, 1)
    behind = pltpu.roll(values, ROT // 2, 1)
    turned = jnp.where(lane < ROT // 2, -ahead, behind)
    return jnp.where(lane < ROT, values * cosine + turned * sine, values)


def forward_kernel(
    place, normed, weights, columns, bias, cosine, sine, starts,
    scaled, q_s, k_s, v_s, out, stats, active, slope, r0, r1, r2, r3,
):
    base = bias[...]
    for r in range(0, D, 128):
        rows = pl.ds(r, 128)
        w = weights[rows, 0:MIXED].astype(full)
        col = columns[rows, :]
        gain_one, shift_one, gain_two, shift_two = (col[:, i : i + 1] for i in range(4))
        w_up, w_qkv = w[:, :UP], w[:, UP:]
        scaled[rows, :] = jnp.concatenate([gain_two * w_up, gain_one * w_qkv], axis=1).astype(low)
        base += jnp.concatenate(
            [jnp.sum(shift_two * w_up, axis=0, keepdims=True), jnp.sum(shift_one * w_qkv, axis=0, keepdims=True)], axis=1
        )

    def project(block, carry):
        rows = pl.ds(pl.multiple_of(block * BLOCK, BLOCK), BLOCK)
        projected = dot(normed[rows, :], scaled[:, AT_QKV:MIXED]) + base[:, AT_QKV:MIXED]
        q_s[rows, :] = (turn(projected[:, 0:WIDTH], cosine[rows, :], sine[rows, :]).astype(low) * (HD**-0.5)).astype(low)
        k_s[rows, :] = turn(projected[:, WIDTH : 2 * WIDTH], cosine[rows, :], sine[rows, :]).astype(low)
        v_s[rows, :] = projected[:, 2 * WIDTH : 3 * WIDTH].astype(low)
        return carry

    lax.fori_loop(0, SEQ // BLOCK, project, 0)
    for block in range(SEQ // BLOCK):
        rows = pl.ds(block * BLOCK, BLOCK)
        allowed = allowed_keys(block, starts)
        keys = (block + 1) * BLOCK
        for head in range(HEADS):
            lanes = pl.ds(head * HD, HD)
            scores = jnp.where(allowed, dot(q_s[rows, lanes], k_s[0:keys, lanes], NT), -1e30)
            most = jnp.max(scores, axis=-1, keepdims=True)
            expo = jnp.exp(scores - most)
            size = jnp.sum(expo, axis=-1, keepdims=True)
            attended = dot((expo * (1.0 / size)).astype(low), v_s[0:keys, lanes])
            out[rows, lanes] = attended
            stats[rows, head : head + 1] = most + jnp.log(size)
    half = UP // 2

    def feed(i, carry):
        rows = pl.ds(pl.multiple_of(i * BLOCK, BLOCK), BLOCK)
        for j in range(2):
            cols = slice(j * half, (j + 1) * half)
            hidden = dot(normed[rows, :], scaled[:, cols]) + base[:, cols]
            gate = 0.5 * (1.0 + lax.erf(hidden * (0.5**0.5)))
            active[rows, cols] = (hidden * gate).astype(low)
            slope[rows, cols] = gate + hidden * jnp.exp(-0.5 * hidden * hidden) * (1.0 / math.sqrt(2.0 * math.pi))
        return carry

    lax.fori_loop(0, SEQ // BLOCK, feed, 0)
    for step, part in enumerate((r0, r1, r2, r3)):
        for far in range(2):
            spot = pl.ds(pl.multiple_of(spot_of(place[0], far, step) * ROWS, ROWS), ROWS)
            left = jnp.concatenate([out[spot, :].astype(low), active[spot, :]], axis=1)
            part[far * ROWS : (far + 1) * ROWS, :] = dot(left, weights[:, AT_OUT:AT_EXTRA], NT).astype(low)


def allowed_keys(block, starts):
    keys = (block + 1) * BLOCK
    row_index = block * BLOCK + lax.broadcasted_iota(jnp.int32, (BLOCK, keys), 0)
    key_index = lax.broadcasted_iota(jnp.int32, (BLOCK, keys), 1)
    return (key_index <= row_index) & (key_index >= starts[block * BLOCK : keys, :])


def split_cores(core, rows):
    blocks = rows.reshape(rows.shape[0] // 128, 2, 64, rows.shape[1])
    mine = jnp.where(core == 0, blocks[:, 0], blocks[:, 1])
    others = jnp.where(core == 0, blocks[:, 1], blocks[:, 0])
    return mine.astype(low), others.astype(low)


def feed_backward_kernel(
    core, dy, dy_t, normed_t, columns, weights, out, active, slope,
    d_hidden, do_s, stats, total, keep, send, sums,
):
    half = UP // 2

    def back(i, totals):
        rows = pl.ds(pl.multiple_of(i * BLOCK, BLOCK), BLOCK)
        new = []
        for j in range(2):
            cols = slice(j * half, (j + 1) * half)
            d_active = dot(dy[rows, :], weights[:, AT_DOWN + j * half : AT_DOWN + (j + 1) * half])
            d_low = (d_active * slope[rows, cols]).astype(low)
            d_hidden[rows, cols] = d_low
            new.append(totals[j] + jnp.sum(d_low.astype(full), axis=0, keepdims=True))
        d_out = dot(dy[rows, :], weights[:, AT_OUT : AT_OUT + OUT]).astype(low)
        do_s[rows, :] = d_out
        product = d_out.astype(full) * out[rows, :]
        for head in range(HEADS):
            stats[rows, head : head + 1] = jnp.sum(product[:, head * HD : (head + 1) * HD], axis=-1, keepdims=True)
        return tuple(new)

    totals = lax.fori_loop(0, SEQ // BLOCK, back, (jnp.zeros((1, half), full),) * 2)
    hidden_total = jnp.concatenate(totals, axis=1)
    total[...] = hidden_total

    def step(i, carry):
        rows = pl.ds(pl.multiple_of(i * BLOCK, BLOCK), BLOCK)
        places = pl.ds(i * (BLOCK // 128), BLOCK // 128)
        col = columns[rows, :]
        up_core = dot(normed_t[rows, :], d_hidden[...])
        w_up = weights[rows, AT_UP : AT_UP + UP].astype(full)
        sums[rows, 0:1] = jnp.sum(w_up * up_core, axis=1, keepdims=True)
        sums[rows, 1:2] = jnp.sum(w_up * hidden_total, axis=1, keepdims=True)
        grad_up = col[:, 2:3] * up_core + col[:, 3:4] * hidden_total
        grad_down = dot(dy_t[rows, :], active[...])
        grad_out = dot(dy_t[rows, :], out[...].astype(low))
        mine, others = split_cores(core[0], jnp.concatenate([grad_up, grad_down, grad_out], axis=1))
        keep[places, :, :] = mine
        send[places, :, :] = others
        return carry

    lax.fori_loop(0, D // BLOCK, step, 0)


def backward_kernel(
    spots, q_s, k_s, v_s, do_s, stats, deltas, starts, cosine, sine, scaled, d_hidden, normed_t, columns, weights,
    total, keep, send, sums, u0, u1, u2, u3,
    d_projected, dq_s, dk_s, dv_s,
):
    dk_s[...] = jnp.zeros_like(dk_s)
    dv_s[...] = jnp.zeros_like(dv_s)
    for block in range(SEQ // BLOCK):
        rows = pl.ds(block * BLOCK, BLOCK)
        allowed = allowed_keys(block, starts)
        keys = (block + 1) * BLOCK
        for head in range(HEADS):
            lanes = pl.ds(head * HD, HD)
            q = q_s[rows, lanes]
            k = k_s[0:keys, lanes]
            d_o = do_s[rows, lanes]
            scores = jnp.where(allowed, dot(q, k, NT), -1e30)
            weight = jnp.exp(scores - stats[rows, head : head + 1])
            d_weight = dot(d_o, v_s[0:keys, lanes], NT)
            d_scores = (weight * (d_weight - deltas[rows, head : head + 1])).astype(low)
            dq_s[rows, lanes] = dot(d_scores, k) * (HD**-0.5)
            dk_s[0:keys, lanes] += dot(d_scores, q, TN)
            dv_s[0:keys, lanes] += dot(weight.astype(low), d_o, TN)
    sum_projected = jnp.zeros((1, QKV), full)
    for block in range(SEQ // BLOCK):
        rows = pl.ds(block * BLOCK, BLOCK)
        back = jnp.concatenate(
            [
                turn(dq_s[rows, :], cosine[rows, :], -sine[rows, :]),
                turn(dk_s[rows, :], cosine[rows, :], -sine[rows, :]),
                dv_s[rows, :],
            ],
            axis=1,
        ).astype(low)
        d_projected[rows, :] = back
        sum_projected += jnp.sum(back.astype(full), axis=0, keepdims=True)
    total[...] = sum_projected

    def gradients(i, carry):
        rows = pl.ds(pl.multiple_of(i * BLOCK, BLOCK), BLOCK)
        places = pl.ds(i * (BLOCK // 128), BLOCK // 128)
        col = columns[rows, :]
        core_grad = dot(normed_t[rows, :], d_projected[...])
        w_qkv = weights[rows, AT_QKV:MIXED].astype(full)
        sums[rows, 0:1] = jnp.sum(w_qkv * core_grad, axis=1, keepdims=True)
        sums[rows, 1:2] = jnp.sum(w_qkv * sum_projected, axis=1, keepdims=True)
        mine, others = split_cores(spots[1], col[:, 0:1] * core_grad + col[:, 1:2] * sum_projected)
        keep[places, :, :] = mine
        send[places, :, :] = others
        return carry

    lax.fori_loop(0, D // BLOCK, gradients, 0)
    for step, part in enumerate((u0, u1, u2, u3)):
        for far in range(2):
            spot = pl.ds(pl.multiple_of(spot_of(spots[0], far, step) * ROWS, ROWS), ROWS)
            left = jnp.concatenate([d_hidden[spot, :], d_projected[spot, :]], axis=1)
            part[far * ROWS : (far + 1) * ROWS, :] = dot(left, scaled[...], NT).astype(low)


def shift_rows(parts):
    return (parts[0], along(parts[1], 1), along(parts[2], 2), along(parts[3], -1))


def sum_rows(parts):
    total = sum(part.astype(full) for part in parts)
    return total[:ROWS], total[ROWS:].astype(low)


def local(
    inputs, segments, cotangent, qkv_weight, out_weight, up_weight, down_weight, vectors,
    qkv_first, qkv_second, out_first, out_second, up_first, up_second, down_first, down_second, vec_first, vec_second,
):
    place = lax.axis_index("ctx")
    rank = lax.axis_index("dp")
    place_one = place.reshape(1).astype(jnp.int32)
    core = lax.rem(rank, 2)
    core_one = core.reshape(1).astype(jnp.int32)
    tokens = inputs[0]
    upstream = cotangent[0]

    far_tokens = across(tokens)

    padded = jnp.pad(vectors.reshape(1, 104), ((0, 0), (0, EXTRA - 104)))
    (parcel,) = call(
        pack_kernel, "pack", [((TP, 8, PARCEL), low)], [VMEM] * 6,
        (qkv_weight, out_weight, up_weight, down_weight, padded, segments),
    )
    parcel, far_tokens, upstream = lax.optimization_barrier((parcel, far_tokens, upstream))
    parcel = lax.all_to_all(parcel, "ctx", 0, 0, tiled=True)

    def rows_of(value, far_value):
        pair = jnp.concatenate([value, far_value], axis=0)
        return (pair, along(pair, -1), along(pair, 2), along(pair, 1))

    x_pieces = rows_of(tokens, far_tokens)
    dy_pieces = rows_of(upstream, across(upstream))
    marks = parcel[:, 1, AT_EXTRA:PARCEL].astype(full)
    weights = lax.all_gather(parcel.reshape(64, PARCEL), "dp", axis=0, tiled=True)

    table = ((SEQ, WIDTH), full)
    starts, cosine, sine = call(starts_kernel, "starts", [((SEQ, 1), jnp.int32), table, table], [VMEM], (marks,))

    square = ((SEQ, D), low)
    normed, normed_t = call(
        norm_kernel, "norm", [square, square], [SMEM] + [VMEM] * 4, (place_one,) + x_pieces
    )
    weights, normed, normed_t, starts, cosine, sine = lax.optimization_barrier(
        (weights, normed, normed_t, starts, cosine, sine)
    )
    vec = weights[:, AT_EXTRA : AT_EXTRA + 104].reshape(128, 8, 104)[:, 0].reshape(-1).astype(full)
    columns = vec[: 4 * D].reshape(4, D).T
    bias_qkv = lax.dynamic_slice(vec, (4 * D + QKV * place,), (QKV,)).reshape(HEADS, 3, HD).transpose(1, 0, 2).reshape(QKV)
    bias_up = lax.dynamic_slice(vec, (8 * D + UP * place,), (UP,))
    bias = jnp.concatenate([bias_up, bias_qkv])[None]
    bias_out = vec[7 * D : 8 * D] + vec[12 * D : 13 * D]

    head_rows = ((SEQ, WIDTH), low)
    pairs = ((2 * ROWS, D), low)
    scaled, q, k, v, attended, stats, active, slope, *r_parts = call(
        forward_kernel, "forward",
        [
            ((D, MIXED), low), head_rows, head_rows, head_rows, ((SEQ, WIDTH), full), ((SEQ, HEADS), full),
            ((SEQ, UP), low), ((SEQ, UP), full), pairs, pairs, pairs, pairs,
        ],
        [SMEM] + [VMEM] * 7,
        (place_one, normed, weights, columns, bias, cosine, sine, starts),
    )
    r_parts, dy_pieces = lax.optimization_barrier((r_parts, dy_pieces))
    dy, dy_t = call(
        collect_kernel, "collect", [square, square], [SMEM] + [VMEM] * 4, (place_one,) + dy_pieces
    )
    r_parts = shift_rows(r_parts)

    d_hidden, d_out, deltas, hidden_total, keep, send, sums_two = call(
        feed_backward_kernel, "feed_backward",
        [
            ((SEQ, UP), low), head_rows, ((SEQ, HEADS), full), ((1, UP), full),
            ((8, 64, FEED), low), ((8, 64, FEED), low), ((D, 2), full),
        ],
        [SMEM] + [VMEM] * 8,
        (core_one, dy, dy_t, normed_t, columns, weights, attended, active, slope),
    )
    feed_sum = (keep.astype(full) + other_core(send).astype(full)).astype(low)
    d_out, feed_sum = lax.optimization_barrier((d_out, feed_sum))
    lanes = [[(zl * 2 + k) for zl in range(8)] for k in range(2)]
    feed_parts = lax.all_to_all(feed_sum, "dp", 0, 0, axis_index_groups=lanes, tiled=True)

    projected_total, keep, send, sums_one, *u_parts = call(
        backward_kernel, "backward",
        [((1, QKV), full), ((8, 64, QKV), low), ((8, 64, QKV), low), ((D, 2), full), pairs, pairs, pairs, pairs],
        [SMEM] + [VMEM] * 14,
        (
            jnp.concatenate([place_one, core_one]), q, k, v, d_out, stats, deltas, starts, cosine, sine, scaled, d_hidden,
            normed_t, columns, weights,
        ),
        scratch=[pltpu.VMEM((SEQ, QKV), low)] + [pltpu.VMEM((SEQ, WIDTH), full)] * 3,
    )
    u_parts, send, r_parts, feed_parts = lax.optimization_barrier((u_parts, send, r_parts, feed_parts))
    result, result_far = sum_rows(r_parts)
    result = result + across(result_far).astype(full)
    u_parts = shift_rows(u_parts)

    upstream_total = jnp.sum(upstream.astype(full), axis=0)
    grad_bias_qkv = projected_total.reshape(3, HEADS, HD).transpose(1, 0, 2).reshape(QKV)
    grad_vectors = jnp.concatenate(
        [
            jnp.concatenate([sums_one, sums_two], axis=1).T.reshape(-1),
            lax.dynamic_update_slice(jnp.zeros((3 * D,), full), grad_bias_qkv, (QKV * place,)),
            upstream_total,
            lax.dynamic_update_slice(jnp.zeros((FF,), full), hidden_total[0], (UP * place,)),
            upstream_total,
        ]
    )
    grad_vectors = jnp.pad(grad_vectors.reshape(8, 2, TP, 1, 104), ((0, 0), (0, 0), (0, 0), (0, 7), (0, EXTRA - 104)))
    grad_vectors = grad_vectors.astype(low).reshape(8, 2, 64, EXTRA)
    vec_keep = jnp.where(core == 0, grad_vectors[:, 0], grad_vectors[:, 1])
    vec_send = jnp.where(core == 0, grad_vectors[:, 1], grad_vectors[:, 0])
    rest_got = other_core(jnp.concatenate([send, vec_send], axis=2))
    rest_sum = (jnp.concatenate([keep, vec_keep], axis=2).astype(full) + rest_got.astype(full)).astype(low)
    rest_parts = lax.all_to_all(rest_sum, "dp", 0, 0, axis_index_groups=lanes, tiled=True)
    u_parts, rest_parts = lax.optimization_barrier((u_parts, rest_parts))
    d_own, d_far = sum_rows(u_parts)
    d_own = d_own + across(d_far).astype(full)
    rest_rows = jnp.sum(rest_parts.astype(full), axis=0).astype(low).reshape(TP, 8, QKV + EXTRA)
    feed_rows = jnp.sum(feed_parts.astype(full), axis=0).astype(low).reshape(TP, 8, FEED)
    own_rows = jnp.concatenate([feed_rows, rest_rows], axis=2)
    own_grads = lax.all_to_all(own_rows, "ctx", 0, 0, tiled=True)

    outputs = tokens.astype(full) + result + bias_out
    own, rate = normalise(tokens.astype(full))
    d_tokens = rate * (
        d_own - jnp.mean(d_own, axis=-1, keepdims=True) - own * jnp.mean(d_own * own, axis=-1, keepdims=True)
    )
    input_grad = upstream.astype(full) + d_tokens

    feed_grads = own_grads[:, :, :FEED].astype(full)
    rest_grads = own_grads[:, :, FEED:].astype(full)
    up_grad = feed_grads[:, :, :UP].transpose(1, 0, 2).reshape(8, FF)
    down_grad = feed_grads[:, :, UP : 2 * UP].transpose(1, 0, 2).reshape(8, FF)
    out_grad = feed_grads[:, :, 2 * UP :].transpose(1, 0, 2).reshape(8, D)
    qkv_grad = rest_grads[:, :, :QKV].reshape(TP, 8, 3, HEADS, HD).transpose(1, 0, 3, 2, 4).reshape(8, 3 * D)
    vector_grad = jnp.sum(rest_grads[:, 0, QKV : QKV + 104], axis=0)

    qkv_new = adamw(qkv_weight, qkv_first, qkv_second, qkv_grad, 2.0 / math.sqrt(D), 0.1)
    out_new = adamw(out_weight, out_first, out_second, out_grad, 8.0 / math.sqrt(D), 0.1)
    up_new = adamw(up_weight, up_first, up_second, up_grad, 2.0 / math.sqrt(D), 0.1)
    down_new = adamw(down_weight, down_first, down_second, down_grad, 2.0 / math.sqrt(FF), 0.1)
    vec_new = adamw(vectors, vec_first, vec_second, vector_grad, 0.5, 0.0)
    return (outputs.astype(low)[None], input_grad[None]) + qkv_new + out_new + up_new + down_new + vec_new


def solution(mesh):
    tokens = P("dp", "ctx", None)
    matrix = P(("dp", "ctx"), None)
    vector = P(("dp", "ctx"))
    return jax.shard_map(
        local,
        mesh=mesh,
        in_specs=(tokens, P("dp", "ctx"), tokens) + (matrix,) * 4 + (vector,) + (matrix,) * 8 + (vector,) * 2,
        out_specs=(tokens, tokens) + (matrix,) * 12 + (vector,) * 3,
        check_vma=False,
    )
```

```python
import math

import jax
import jax.numpy as jnp
import numpy as np
from jax import lax
from jax.experimental import pallas as pl
from jax.experimental.pallas import tpu as pltpu
from jax.sharding import PartitionSpec as P

D = 1024
H = 16
FF = 4096
HD = 64
ROT = 16
STEP = 10
SEQ = 1024
TP = 8
ROWS = SEQ // TP
HEADS = H // TP
WIDTH = HEADS * HD
QKV = 3 * D // TP
OUT = D // TP
UP = FF // TP
EXTRA = 128
MIXED = UP + QKV
FEED = 2 * UP + OUT
REST = QKV + EXTRA
BLOCK = 256

beta_one = 0.9
beta_two = 0.95
epsilon = 1e-08
norm_epsilon = 1e-05
FREQUENCIES = [float(f) for f in 10000.0 ** (-np.arange(ROT // 2, dtype=np.float32) * np.float32(2.0) / np.float32(ROT))]
low = jnp.bfloat16
full = jnp.float32

AT_UP = 0
AT_QKV = UP
AT_OUT = UP + QKV
AT_DOWN = AT_OUT + OUT
AT_EXTRA = AT_DOWN + UP
PARCEL = AT_EXTRA + EXTRA
AT_START = 2 * ROT
AT_SIZE = AT_START + 1

NT = ((1,), (1,))
TN = ((0,), (0,))
VMEM = pl.BlockSpec(memory_space=pltpu.VMEM)
SMEM = pl.BlockSpec(memory_space=pltpu.SMEM)


def dot(a, b, dims=((1,), (0,))):
    return lax.dot_general(a, b, (dims, ((), ())), preferred_element_type=full)


FAR = pl.BlockSpec(memory_space=pltpu.HBM)
NEAR = pl.BlockSpec(memory_space=pltpu.VMEM)


def call(kernel, name, results, operands, scratch=(), copies=0, limit=40):
    spaces = {id(VMEM): pltpu.VMEM, id(FAR): pltpu.HBM, id(NEAR): jax.ShapeDtypeStruct}

    def held(operand, spec):
        return operand if spec is SMEM else pltpu.with_memory_space_constraint(operand, spaces[id(spec)])

    return pl.pallas_call(
        kernel,
        out_shape=tuple(spaces[id(spec)](*s) for s, spec in results),
        in_specs=[spec for _, spec in operands],
        out_specs=tuple(spec for _, spec in results),
        scratch_shapes=[pltpu.VMEM(*s) for s in scratch] + [pltpu.SemaphoreType.DMA((copies,))] * (copies > 0),
        compiler_params=pltpu.CompilerParams(vmem_limit_bytes=limit * 2**20),
        cost_estimate=pl.CostEstimate(flops=1024, bytes_accessed=1024, transcendentals=0),
        name=name,
    )(*(held(*o) for o in operands))


class Mover:
    def __init__(self, semaphores):
        self.semaphores, self.used, self.leaving = semaphores, 0, []

    def start(self, source, target):
        copy = pltpu.make_async_copy(source, target, self.semaphores.at[self.used])
        self.used += 1
        copy.start()
        return copy

    def send(self, source, target):
        self.leaving.append(self.start(source, target))

    def finish(self):
        for copy in self.leaving:
            copy.wait()


def adamw(weight, moment_one, moment_two, gradient, step_rate, decay_rate):
    moment_one = beta_one * moment_one + (1.0 - beta_one) * gradient
    moment_two = beta_two * moment_two + (1.0 - beta_two) * gradient * gradient
    fix_one = 1.0 - beta_one**STEP
    fix_two = 1.0 - beta_two**STEP
    update = moment_one / fix_one / (jnp.sqrt(moment_two / fix_two) + epsilon)
    weight = weight - step_rate * (update + decay_rate * weight)
    return (weight, moment_one, moment_two)


def normalise(values):
    center = values - jnp.mean(values, axis=-1, keepdims=True)
    spread = jnp.mean(center * center, axis=-1, keepdims=True)
    rate = lax.rsqrt(spread + norm_epsilon)
    return center * rate, rate


def across(value):
    return lax.ppermute(value, "ctx", [(i, (i + 4) % 8) for i in range(8)])


def along(value, step):
    return lax.ppermute(value, "ctx", [(a * 4 + b, a * 4 + (b + step) % 4) for a in range(2) for b in range(4)])


def other_core(value):
    return lax.ppermute(value, "dp", [(i, i ^ 1) for i in range(16)])


def spot_of(place, far, step):
    half, row = place // 4, place % 4
    half = 1 - half if far else half
    return half * 4 + (row + step) % 4


def pack_kernel(place, qkv, out, up, down, vec, marks, near, far, qkv_s, out_s, up_s, down_s, semaphores):
    move = Mover(semaphores)
    arriving = [move.start(*p) for p in ((qkv, qkv_s), (out, out_s), (up, up_s), (down, down_s))]
    extra = jnp.concatenate([vec[...], marks[...].astype(full), jnp.zeros((6, EXTRA), full)], axis=0).astype(low)
    for copy in arriving:
        copy.wait()
    for is_far, parcel in ((1, far), (0, near)):
        for step in range(4):
            c = spot_of(place[0], is_far, step)
            cut = qkv_s[:, pl.ds(pl.multiple_of(c * QKV, 128), QKV)].astype(low)
            parts = [cut[:, (h * 3 + p) * HD : (h * 3 + p + 1) * HD] for p in range(3) for h in range(HEADS)]
            parcel[step, :, AT_QKV:AT_OUT] = jnp.concatenate(parts, axis=1)
            parcel[step, :, AT_UP : AT_UP + UP] = up_s[:, pl.ds(pl.multiple_of(c * UP, 128), UP)].astype(low)
            parcel[step, :, AT_OUT : AT_OUT + OUT] = out_s[:, pl.ds(pl.multiple_of(c * OUT, 128), OUT)].astype(low)
            parcel[step, :, AT_DOWN : AT_DOWN + UP] = down_s[:, pl.ds(pl.multiple_of(c * UP, 128), UP)].astype(low)
            parcel[step, :, AT_EXTRA:PARCEL] = extra


def regroup_kernel(near, far, *refs):
    for step in range(4):
        refs[step][0] = near[step]
        refs[step][1] = far[step]


def assemble_kernel(place, *refs):
    pieces, whole = refs[:4], refs[4]
    for step in range(4):
        for far in range(2):
            whole[pl.ds(spot_of(place[0], far, step), 1)] = pieces[step][far : far + 1]


def starts_kernel(marks, table, staged, semaphores):
    move = Mover(semaphores)
    whole = marks[...]
    start = jnp.zeros_like(whole)
    for k in range(1, 8):
        start = jnp.where(whole == k, jnp.sum((whole < k).astype(full), keepdims=True), start)
    row = lax.broadcasted_iota(jnp.int32, whole.shape, 0) * ROWS + lax.broadcasted_iota(jnp.int32, whole.shape, 1)
    positions = row.astype(full) - start
    slow = lax.broadcasted_iota(jnp.int32, (ROT // 2, 1), 0)
    frequency = jnp.zeros((ROT // 2, 1), full)
    for i, value in enumerate(FREQUENCIES):
        frequency = jnp.where(slow == i, value, frequency)
    turned = start.T
    for block in range(TP):
        rows = slice(block * ROWS, (block + 1) * ROWS)
        angles = positions[block : block + 1, :] * frequency
        cos_one = jnp.cos(angles).T
        sin_one = jnp.sin(angles).T
        start_one = jnp.broadcast_to(turned[:, block : block + 1], (ROWS, WIDTH - 2 * ROT))
        staged[rows, :] = jnp.concatenate([cos_one, cos_one, sin_one, sin_one, start_one], axis=1)
    move.send(staged, table)
    move.finish()


def norm_kernel(place, *refs):
    pieces, (whole, stored, staged, semaphores) = refs[:4], refs[4:]
    move = Mover(semaphores)
    arriving = [move.start(pieces[step], staged.at[step]) for step in range(4)]
    for step in range(4):
        arriving[step].wait()
        for far in range(2):
            spot = pl.multiple_of(spot_of(place[0], far, step) * ROWS, ROWS)
            normed, _ = normalise(staged[step, far * ROWS : (far + 1) * ROWS, :].astype(full))
            whole[pl.ds(spot, ROWS), :] = normed.astype(low)
    move.send(whole, stored)
    move.finish()


def angles_of(table):
    lane = lax.broadcasted_iota(jnp.int32, table.shape, 1)
    sine = pltpu.roll(table, WIDTH - ROT, 1)
    return tuple(jnp.where(lane < HD, t, pltpu.roll(t, HD, 1)) for t in (table, sine))


def turn(values, cosine, sine):
    lane = lax.broadcasted_iota(jnp.int32, values.shape, 1) % HD
    ahead = pltpu.roll(values, values.shape[1] - ROT // 2, 1)
    behind = pltpu.roll(values, ROT // 2, 1)
    turned = jnp.where(lane < ROT // 2, -ahead, behind)
    return jnp.where(lane < ROT, values * cosine + turned * sine, values)


def allowed_keys(block, starts):
    keys = (block + 1) * BLOCK
    row_index = block * BLOCK + lax.broadcasted_iota(jnp.int32, (BLOCK, keys), 0)
    key_index = lax.broadcasted_iota(jnp.int32, (BLOCK, keys), 1)
    return (key_index <= row_index) & (key_index >= starts.astype(jnp.int32))


def split_cores(core, rows):
    blocks = rows.reshape(rows.shape[0] // 128, 2, 64, rows.shape[1])
    mine = jnp.where(core == 0, blocks[:, 0], blocks[:, 1])
    others = jnp.where(core == 0, blocks[:, 1], blocks[:, 0])
    return mine.astype(low), others.astype(low)


def forward_kernel(
    place, normed, columns, bias, weights, table,
    attended_out, active_out, slope_out, scaled_out, qkv_out, table_out, r0, r1, r2, r3,
    w_s, table_s, scaled, qkv, part_s, attended, active, slope, semaphores,
):
    move = Mover(semaphores)
    step_rows = 256
    arriving = [
        move.start(weights.at[pl.ds(r, step_rows), pl.ds(0, MIXED)], w_s.at[pl.ds(r, step_rows), pl.ds(0, MIXED)])
        for r in range(0, D, step_rows)
    ]
    base = bias[...]
    for r in range(0, D, 128):
        if r % step_rows == 0:
            arriving[r // step_rows].wait()
        if r == D // 2:
            table_arrives = move.start(table, table_s)
            rest_arrives = move.start(weights.at[:, pl.ds(MIXED, OUT + UP)], w_s.at[:, pl.ds(MIXED, OUT + UP)])
        rows = pl.ds(r, 128)
        w = w_s[rows, 0:MIXED].astype(full)
        col = columns[rows, :]
        gain_one, shift_one, gain_two, shift_two = (col[:, i : i + 1] for i in range(4))
        w_up, w_qkv = w[:, :UP], w[:, UP:]
        scaled[rows, :] = jnp.concatenate([gain_two * w_up, gain_one * w_qkv], axis=1).astype(low)
        base += jnp.concatenate(
            [jnp.sum(shift_two * w_up, axis=0, keepdims=True), jnp.sum(shift_one * w_qkv, axis=0, keepdims=True)], axis=1
        )
    move.send(scaled, scaled_out)
    table_arrives.wait()

    def project(block, carry):
        rows = pl.ds(pl.multiple_of(block * BLOCK, BLOCK), BLOCK)
        projected = dot(normed[rows, :], scaled[:, AT_QKV:MIXED]) + base[:, AT_QKV:MIXED]
        cosine, sine = angles_of(table_s[rows, :])
        q = (turn(projected[:, 0:WIDTH], cosine, sine).astype(low) * (HD**-0.5)).astype(low)
        k = turn(projected[:, WIDTH : 2 * WIDTH], cosine, sine).astype(low)
        v = projected[:, 2 * WIDTH : 3 * WIDTH].astype(low)
        qkv[rows, :] = jnp.concatenate([q, k, v], axis=1)
        return carry

    lax.fori_loop(0, SEQ // BLOCK, project, 0)
    move.send(qkv, qkv_out)
    for block in range(SEQ // BLOCK):
        rows = pl.ds(block * BLOCK, BLOCK)
        allowed = allowed_keys(block, table_s[rows, AT_START : AT_START + 1])
        keys = (block + 1) * BLOCK
        for head in range(HEADS):
            at = head * HD
            q = qkv[rows, at : at + HD]
            k = qkv[0:keys, WIDTH + at : WIDTH + at + HD]
            v = qkv[0:keys, 2 * WIDTH + at : 2 * WIDTH + at + HD]
            scores = jnp.where(allowed, dot(q, k, NT), -1e30)
            most = jnp.max(scores, axis=-1, keepdims=True)
            expo = jnp.exp(scores - most)
            size = jnp.sum(expo, axis=-1, keepdims=True)
            attended[rows, at : at + HD] = dot((expo * (1.0 / size)).astype(low), v).astype(low)
            table_s[rows, AT_SIZE + head : AT_SIZE + head + 1] = most + jnp.log(size)
    move.send(attended, attended_out)
    move.send(table_s, table_out)
    half = UP // 2

    def feed(i, carry):
        rows = pl.ds(pl.multiple_of(i * BLOCK, BLOCK), BLOCK)
        for j in range(2):
            cols = slice(j * half, (j + 1) * half)
            hidden = dot(normed[rows, :], scaled[:, cols]) + base[:, cols]
            gate = 0.5 * (1.0 + lax.erf(hidden * (0.5**0.5)))
            active[rows, cols] = (hidden * gate).astype(low)
            inner = gate + hidden * jnp.exp(-0.5 * hidden * hidden) * (1.0 / math.sqrt(2.0 * math.pi))
            slope[rows, cols] = inner.astype(low)
        return carry

    lax.fori_loop(0, SEQ // BLOCK, feed, 0)
    move.send(active, active_out)
    move.send(slope, slope_out)
    rest_arrives.wait()
    for step, part in enumerate((r0, r1, r2, r3)):
        spots = [pl.ds(pl.multiple_of(spot_of(place[0], far, step) * ROWS, ROWS), ROWS) for far in range(2)]
        left = [jnp.concatenate([attended[spot, :], active[spot, :]], axis=1) for spot in spots]
        part_s[step] = dot(jnp.concatenate(left, axis=0), w_s[:, AT_OUT:AT_EXTRA], NT).astype(low)
        move.send(part_s.at[step], part)
    move.finish()


def backward_kernel(
    spots, upstream_total, attended_far, active_far, slope_far, dy0, dy1, dy2, dy3, normed, columns, weights, table, qkv, scaled,
    keep, send, u0, u1, u2, u3,
    dy, w_s, normed_s, col_s, table_s, qkv_s, scaled_s, mixed, do_s, kept_s, sums, dq_s, dk_s, dv_s, keep_s, send_s, part_s, early,
    attended, active, slope, semaphores,
):
    move = Mover(semaphores)
    down_arrives = move.start(weights.at[:, pl.ds(AT_OUT, OUT + UP)], w_s.at[:, pl.ds(AT_OUT, OUT + UP)])
    dy_arrive = []
    for step, piece in enumerate((dy0, dy1, dy2, dy3)):
        for far in range(2):
            spot = pl.multiple_of(spot_of(spots[0], far, step) * ROWS, ROWS)
            dy_arrive.append(move.start(piece.at[pl.ds(far * ROWS, ROWS)], dy.at[pl.ds(spot, ROWS)]))
    held_arrive = [move.start(*p) for p in ((slope_far, slope), (attended_far, attended))]
    half = UP // 2
    down_arrives.wait()
    for copy in held_arrive:
        copy.wait()
    table_arrives = move.start(table, table_s)
    qkv_arrives = move.start(qkv, qkv_s)
    scaled_arrives = move.start(scaled, scaled_s)
    totals = [jnp.zeros((1, half), full)] * 2
    later = []
    for step in range(4):
        for copy in dy_arrive[2 * step : 2 * step + 2]:
            copy.wait()
        at = [pl.ds(pl.multiple_of(spot_of(spots[0], far, step) * ROWS, ROWS), ROWS) for far in range(2)]
        dy_now = jnp.concatenate([dy[rows, :] for rows in at], axis=0)
        for j in range(2):
            cols = slice(j * half, (j + 1) * half)
            d_active = dot(dy_now, w_s[:, AT_DOWN + j * half : AT_DOWN + (j + 1) * half])
            d_low = (d_active * jnp.concatenate([slope[rows, cols] for rows in at], axis=0).astype(full)).astype(low)
            for far in range(2):
                mixed[at[far], cols] = d_low[far * ROWS : (far + 1) * ROWS]
            totals[j] += jnp.sum(d_low.astype(full), axis=0, keepdims=True)
        d_out = dot(dy_now, w_s[:, AT_OUT : AT_OUT + OUT]).astype(low)
        for far in range(2):
            d_now = d_out[far * ROWS : (far + 1) * ROWS]
            do_s[at[far], :] = d_now
            product = d_now.astype(full) * attended[at[far], :].astype(full)
            for h in range(HEADS):
                kept_s[at[far], h : h + 1] = jnp.sum(product[:, h * HD : (h + 1) * HD], axis=-1, keepdims=True)
        if step == 0:
            later = [
                move.start(*p)
                for p in (
                    (normed, normed_s), (active_far, active), (columns, col_s),
                    (weights.at[:, pl.ds(0, MIXED)], w_s.at[:, pl.ds(0, MIXED)]),
                )
            ]
    hidden_total = jnp.concatenate(totals, axis=1)

    dk_s[...] = jnp.zeros_like(dk_s)
    dv_s[...] = jnp.zeros_like(dv_s)
    table_arrives.wait()
    qkv_arrives.wait()
    for block in range(SEQ // BLOCK):
        rows = pl.ds(block * BLOCK, BLOCK)
        allowed = allowed_keys(block, table_s[rows, AT_START : AT_START + 1])
        keys = (block + 1) * BLOCK
        for head in range(HEADS):
            at = head * HD
            lanes = pl.ds(at, HD)
            q = qkv_s[rows, at : at + HD]
            k = qkv_s[0:keys, WIDTH + at : WIDTH + at + HD]
            v = qkv_s[0:keys, 2 * WIDTH + at : 2 * WIDTH + at + HD]
            d_o = do_s[rows, lanes]
            scores = jnp.where(allowed, dot(q, k, NT), -1e30)
            weight = jnp.exp(scores - table_s[rows, AT_SIZE + head : AT_SIZE + head + 1])
            d_weight = dot(d_o, v, NT)
            d_scores = (weight * (d_weight - kept_s[rows, head : head + 1])).astype(low)
            dq_s[rows, lanes] = dot(d_scores, k) * (HD**-0.5)
            dk_s[0:keys, lanes] += dot(d_scores, q, TN)
            dv_s[0:keys, lanes] += dot(weight.astype(low), d_o, TN)
    total = jnp.zeros((1, QKV), full)
    for block in range(SEQ // BLOCK):
        rows = pl.ds(block * BLOCK, BLOCK)
        cosine, sine = angles_of(table_s[rows, :])
        sine = -sine
        back_low = jnp.concatenate(
            [turn(dq_s[rows, :], cosine, sine), turn(dk_s[rows, :], cosine, sine), dv_s[rows, :]], axis=1
        ).astype(low)
        mixed[rows, AT_QKV:MIXED] = back_low
        total += jnp.sum(back_low.astype(full), axis=0, keepdims=True)

    scaled_arrives.wait()
    for step, part in ((1, u1), (2, u2), (3, u3), (0, u0)):
        left = [mixed[pl.ds(pl.multiple_of(spot_of(spots[0], far, step) * ROWS, ROWS), ROWS), :] for far in range(2)]
        part_s[step] = dot(jnp.concatenate(left, axis=0), scaled_s[...], NT).astype(low)
        move.send(part_s.at[step], part)

    for copy in later:
        copy.wait()
    lane = lax.broadcasted_iota(jnp.int32, (BLOCK, 128), 1)
    mixed_total = jnp.concatenate([hidden_total, total], axis=1)
    for i in range(D // BLOCK):
        rows = pl.ds(i * BLOCK, BLOCK)
        places = pl.ds(i * (BLOCK // 128), BLOCK // 128)
        col = col_s[rows, :]
        core_grad = dot(normed_s[:, rows], mixed[...], TN)
        w_mixed = w_s[rows, 0:MIXED].astype(full)
        gain_terms, shift_terms = w_mixed * core_grad, w_mixed * mixed_total
        found = [jnp.sum(t[:, c], axis=1, keepdims=True) for c in (slice(UP, MIXED), slice(0, UP)) for t in (gain_terms, shift_terms)]
        columns_now = jnp.zeros((BLOCK, 128), full)
        for n in range(4):
            columns_now = jnp.where(lane == n, found[n], columns_now)
        sums[rows, :] = columns_now
        grad_up = col[:, 2:3] * core_grad[:, :UP] + col[:, 3:4] * hidden_total
        grad_qkv = col[:, 0:1] * core_grad[:, UP:] + col[:, 1:2] * total
        grad_down = dot(dy[:, rows], active[...], TN)
        grad_out = dot(dy[:, rows], attended[...], TN)
        mine, others = split_cores(spots[1], jnp.concatenate([grad_up, grad_down, grad_out, grad_qkv], axis=1))
        keep_s[places, :, 0 : FEED + QKV] = mine
        send_s[places, :, 0 : FEED + QKV] = others
        for staged, target in ((send_s, send), (keep_s, keep)):
            done = (places, slice(None), pl.ds(0, FEED + QKV))
            move.send(staged.at[done], target.at[done])
    early[...] = jnp.zeros_like(early)
    for r in range(0, D, 128):
        turned = sums[r : r + 128, :].T
        for n in range(4):
            early[:, n * D + r : n * D + r + 128] = turned[n : n + 1, :]
    bias_total = jnp.concatenate(
        [total[:, part * WIDTH + h * HD : part * WIDTH + (h + 1) * HD] for h in range(HEADS) for part in range(3)], axis=1
    )
    early[:, pl.ds(pl.multiple_of(4 * D + spots[0] * QKV, 128), QKV)] = bias_total
    early[:, 7 * D : 8 * D] = upstream_total[...]
    early[:, pl.ds(pl.multiple_of(8 * D + spots[0] * UP, UP), UP)] = hidden_total
    early[:, 12 * D : 13 * D] = upstream_total[...]
    for zl in range(8):
        parts = []
        for core in range(2):
            lines = []
            for c in range(TP):
                at = ((zl * 2 + core) * TP + c) * 104
                lines.append(jnp.concatenate([early[:, at : at + 104], jnp.zeros((1, EXTRA - 104), full)], axis=1))
                lines.append(jnp.zeros((7, EXTRA), full))
            parts.append(jnp.concatenate(lines, axis=0))
        keep_s[zl, :, FEED + QKV : PARCEL] = jnp.where(spots[1] == 0, parts[0], parts[1]).astype(low)
        send_s[zl, :, FEED + QKV : PARCEL] = jnp.where(spots[1] == 0, parts[1], parts[0]).astype(low)
    for staged, target in ((send_s, send), (keep_s, keep)):
        done = (slice(None), slice(None), pl.ds(FEED + QKV, EXTRA))
        move.send(staged.at[done], target.at[done])
    move.finish()


def update_kernel(grads, *refs):
    state, new = refs[:15], refs[15:30]

    def update(index, columns, gradient, rate, decay):
        results = adamw(*(state[3 * index + i][:, columns] for i in range(3)), gradient.astype(full), rate, decay)
        for i in range(3):
            new[3 * index + i][:, columns] = results[i]

    total = jnp.zeros((1, 104), full)
    for c in range(TP):
        at = FEED
        parts = [[grads[c, :, at + (p * HEADS + h) * HD : at + (p * HEADS + h + 1) * HD] for p in range(3)] for h in range(HEADS)]
        qkv = jnp.concatenate([part for head in parts for part in head], axis=1)
        update(0, slice(c * QKV, (c + 1) * QKV), qkv, 2.0 / math.sqrt(D), 0.1)
        update(1, slice(c * OUT, (c + 1) * OUT), grads[c, :, 2 * UP : FEED], 8.0 / math.sqrt(D), 0.1)
        update(2, slice(c * UP, (c + 1) * UP), grads[c, :, 0:UP], 2.0 / math.sqrt(D), 0.1)
        update(3, slice(c * UP, (c + 1) * UP), grads[c, :, UP : 2 * UP], 2.0 / math.sqrt(FF), 0.1)
        total += grads[c, :, FEED + QKV : FEED + QKV + 104].astype(full)[0:1, :]
    update(4, slice(0, 104), total, 0.5, 0.0)


def shift_rows(parts):
    return (parts[0], along(parts[1], 1), along(parts[2], 2), along(parts[3], -1))


def sum_rows(parts):
    total = sum(part.astype(full) for part in parts)
    return total[:ROWS], total[ROWS:].astype(low)


def local(
    inputs, segments, cotangent, qkv_weight, out_weight, up_weight, down_weight, vectors,
    qkv_first, qkv_second, out_first, out_second, up_first, up_second, down_first, down_second, vec_first, vec_second,
):
    place = lax.axis_index("ctx")
    rank = lax.axis_index("dp")
    place_one = place.reshape(1).astype(jnp.int32)
    core = lax.rem(rank, 2)
    spots = jnp.stack([place, core]).astype(jnp.int32)
    tokens = inputs[0]
    upstream = cotangent[0]

    far_tokens = across(tokens)

    padded = jnp.pad(vectors.reshape(1, 104), ((0, 0), (0, EXTRA - 104)))
    quarter, piece = ((4, 8, PARCEL), low), ((2, 8, PARCEL), low)
    near, far = call(
        pack_kernel, "pack", [(quarter, VMEM)] * 2,
        [(place_one, SMEM)] + [(o, FAR) for o in (qkv_weight, out_weight, up_weight, down_weight)] + [(padded, VMEM), (segments, VMEM)],
        scratch=[((8, n), full) for n in (3 * D, D, FF, FF)], copies=4,
    )
    far, far_tokens = lax.optimization_barrier((across(far), far_tokens))
    sends = call(regroup_kernel, "regroup", [(piece, VMEM)] * 4, [(near, VMEM), (far, VMEM)])
    pieces = (sends[0], along(sends[3], -1), along(sends[2], 2), along(sends[1], 1))
    (parcel,) = call(
        assemble_kernel, "assemble", [(((TP, 8, PARCEL), low), VMEM)], [(place_one, SMEM)] + [(o, VMEM) for o in pieces]
    )

    def rows_of(value, far_value):
        pair = jnp.concatenate([value, far_value], axis=0)
        return (pair, along(pair, -1), along(pair, 2), along(pair, 1))

    x_pieces = rows_of(tokens, far_tokens)
    dy_pieces = rows_of(upstream, across(upstream))
    marks = parcel[:, 1, AT_EXTRA:PARCEL].astype(full)
    weights = lax.all_gather(parcel.reshape(64, PARCEL), "dp", axis=0, tiled=True)

    (table,) = call(
        starts_kernel, "starts", [(((SEQ, WIDTH), full), FAR)], [(marks, VMEM)], scratch=[((SEQ, WIDTH), full)], copies=1
    )
    square = ((SEQ, D), low)
    normed, normed_far = call(
        norm_kernel, "norm", [(square, VMEM), (square, FAR)], [(place_one, SMEM)] + [(o, FAR) for o in x_pieces],
        scratch=[((4, 2 * ROWS, D), low)], copies=5,
    )
    weights, normed, table = lax.optimization_barrier((weights, normed, table))
    vec = weights[:, AT_EXTRA : AT_EXTRA + 104].reshape(128, 8, 104)[:, 0].reshape(-1).astype(full)
    columns = vec[: 4 * D].reshape(4, D).T
    bias_qkv = lax.dynamic_slice(vec, (4 * D + QKV * place,), (QKV,)).reshape(HEADS, 3, HD).transpose(1, 0, 2).reshape(QKV)
    bias_up = lax.dynamic_slice(vec, (8 * D + UP * place,), (UP,))
    bias = jnp.concatenate([bias_up, bias_qkv])[None]
    bias_out = vec[7 * D : 8 * D] + vec[12 * D : 13 * D]

    pairs = ((2 * ROWS, D), low)
    head_rows, table_type, scaled_type, qkv_type, hidden_type = ((SEQ, WIDTH), low), ((SEQ, WIDTH), full), ((D, MIXED), low), ((SEQ, QKV), low), ((SEQ, UP), low)
    attended, active, slope, scaled, qkv, table, *r_parts = call(
        forward_kernel, "forward",
        [(o, FAR) for o in (head_rows, hidden_type, hidden_type, scaled_type, qkv_type, table_type)] + [(pairs, FAR)] * 4,
        [(place_one, SMEM), (normed, VMEM), (columns, VMEM), (bias, VMEM), (weights, FAR), (table, FAR)],
        scratch=[((D, AT_EXTRA), low), table_type, scaled_type, qkv_type, ((4, 2 * ROWS, D), low), head_rows, hidden_type, hidden_type],
        copies=16,
    )
    r_parts = shift_rows(r_parts)

    attended, dy_pieces = lax.optimization_barrier((attended, dy_pieces))
    upstream_total = jnp.sum(upstream.astype(full), axis=0, keepdims=True)
    parcel_type, kept_type = ((8, 64, PARCEL), low), ((SEQ, WIDTH), full)
    keep, send, *u_parts = call(
        backward_kernel, "backward",
        [(parcel_type, FAR)] * 2 + [(pairs, FAR)] * 4,
        [(spots, SMEM), (upstream_total, VMEM)]
        + [(o, FAR) for o in (attended, active, slope) + dy_pieces + (normed_far, columns, weights, table, qkv, scaled)],
        scratch=[
            square, ((D, AT_EXTRA), low), square, ((D, 4), full), table_type, qkv_type, scaled_type,
            ((SEQ, MIXED), low), head_rows, kept_type, kept_type, kept_type, kept_type, kept_type,
            parcel_type, parcel_type, ((4, 2 * ROWS, D), low), ((1, 13 * D), full),
            head_rows, hidden_type, hidden_type,
        ],
        copies=32,
    )
    keep, send, r_parts = lax.optimization_barrier((keep, send, r_parts))
    u_parts = shift_rows(u_parts)
    grads = (keep.astype(full) + other_core(send).astype(full)).astype(low)
    result, result_far = sum_rows(r_parts)
    grads, result_far = lax.optimization_barrier((grads, result_far))
    lanes = [[(zl * 2 + k) for zl in range(8)] for k in range(2)]
    grads = lax.all_to_all(grads, "dp", 0, 0, axis_index_groups=lanes, tiled=True)
    grads = jnp.sum(grads.astype(full), axis=0).astype(low).reshape(TP, 8, PARCEL)
    result_far, grads = lax.optimization_barrier((across(result_far), grads))
    own_grads = lax.all_to_all(grads, "ctx", 0, 0, tiled=True)
    u_parts, _ = lax.optimization_barrier((u_parts, grads))
    d_own, d_far = sum_rows(u_parts)
    d_own = d_own + across(d_far).astype(full)
    result = result + result_far.astype(full)

    outputs = tokens.astype(full) + result + bias_out
    own, rate = normalise(tokens.astype(full))
    d_tokens = rate * (
        d_own - jnp.mean(d_own, axis=-1, keepdims=True) - own * jnp.mean(d_own * own, axis=-1, keepdims=True)
    )
    input_grad = upstream.astype(full) + d_tokens

    state = (
        (qkv_weight, qkv_first, qkv_second), (out_weight, out_first, out_second), (up_weight, up_first, up_second),
        (down_weight, down_first, down_second), tuple(v.reshape(1, 104) for v in (vectors, vec_first, vec_second)),
    )
    state = [array for triple in state for array in triple]
    new = call(
        update_kernel, "update", [((o.shape, full), NEAR) for o in state], [(own_grads, VMEM)] + [(o, VMEM) for o in state]
    )
    return (outputs.astype(low)[None], input_grad[None]) + tuple(new[:12]) + tuple(v.reshape(104) for v in new[12:])


def solution(mesh):
    tokens = P("dp", "ctx", None)
    matrix = P(("dp", "ctx"), None)
    vector = P(("dp", "ctx"))
    return jax.shard_map(
        local,
        mesh=mesh,
        in_specs=(tokens, P("dp", "ctx"), tokens) + (matrix,) * 4 + (vector,) + (matrix,) * 8 + (vector,) * 2,
        out_specs=(tokens, tokens) + (matrix,) * 12 + (vector,) * 3,
        check_vma=False,
    )
```

```python
import math

import jax
import jax.numpy as jnp
import numpy as np
from jax import lax
from jax.experimental import pallas as pl
from jax.experimental.pallas import tpu as pltpu
from jax.sharding import PartitionSpec as P

D = 1024
H = 16
FF = 4096
HD = 64
ROT = 16
STEP = 10
SEQ = 1024
TP = 8
ROWS = SEQ // TP
HEADS = H // TP
WIDTH = HEADS * HD
QKV = 3 * D // TP
OUT = D // TP
UP = FF // TP
EXTRA = 128
MIXED = UP + QKV
FEED = 2 * UP + OUT
REST = QKV + EXTRA
BLOCK = 256

beta_one = 0.9
beta_two = 0.95
epsilon = 1e-08
norm_epsilon = 1e-05
FREQUENCIES = [float(f) for f in 10000.0 ** (-np.arange(ROT // 2, dtype=np.float32) * np.float32(2.0) / np.float32(ROT))]
low = jnp.bfloat16
full = jnp.float32

AT_UP = 0
AT_QKV = UP
AT_OUT = UP + QKV
AT_DOWN = AT_OUT + OUT
AT_EXTRA = AT_DOWN + UP
PARCEL = AT_EXTRA + EXTRA
AT_START = 2 * ROT
AT_SIZE = AT_START + 1
AT_NORMS = AT_SIZE + HEADS

NT = ((1,), (1,))
TN = ((0,), (0,))
VMEM = pl.BlockSpec(memory_space=pltpu.VMEM)
SMEM = pl.BlockSpec(memory_space=pltpu.SMEM)


def dot(a, b, dims=((1,), (0,))):
    return lax.dot_general(a, b, (dims, ((), ())), preferred_element_type=full)


FAR = pl.BlockSpec(memory_space=pltpu.HBM)
NEAR = pl.BlockSpec(memory_space=pltpu.VMEM)


def call(kernel, name, results, operands, scratch=(), copies=0, limit=40):
    spaces = {id(VMEM): pltpu.VMEM, id(FAR): pltpu.HBM, id(NEAR): jax.ShapeDtypeStruct}

    def held(operand, spec):
        return operand if spec is SMEM else pltpu.with_memory_space_constraint(operand, spaces[id(spec)])

    return pl.pallas_call(
        kernel,
        out_shape=tuple(spaces[id(spec)](*s) for s, spec in results),
        in_specs=[spec for _, spec in operands],
        out_specs=tuple(spec for _, spec in results),
        scratch_shapes=[pltpu.VMEM(*s) for s in scratch] + [pltpu.SemaphoreType.DMA((copies,))] * (copies > 0),
        compiler_params=pltpu.CompilerParams(vmem_limit_bytes=limit * 2**20),
        cost_estimate=pl.CostEstimate(flops=1024, bytes_accessed=1024, transcendentals=0),
        name=name,
    )(*(held(*o) for o in operands))


class Mover:
    def __init__(self, semaphores):
        self.semaphores, self.used, self.leaving = semaphores, 0, []

    def start(self, source, target):
        copy = pltpu.make_async_copy(source, target, self.semaphores.at[self.used])
        self.used += 1
        copy.start()
        return copy

    def send(self, source, target):
        self.leaving.append(self.start(source, target))

    def finish(self):
        for copy in self.leaving:
            copy.wait()


def adamw(weight, moment_one, moment_two, gradient, step_rate, decay_rate):
    moment_one = beta_one * moment_one + (1.0 - beta_one) * gradient
    moment_two = beta_two * moment_two + (1.0 - beta_two) * gradient * gradient
    fix_one = 1.0 - beta_one**STEP
    fix_two = 1.0 - beta_two**STEP
    update = moment_one / fix_one / (jnp.sqrt(moment_two / fix_two) + epsilon)
    weight = weight - step_rate * (update + decay_rate * weight)
    return (weight, moment_one, moment_two)


def normalise(values):
    center = values - jnp.mean(values, axis=-1, keepdims=True)
    spread = jnp.mean(center * center, axis=-1, keepdims=True)
    rate = lax.rsqrt(spread + norm_epsilon)
    return center * rate, rate


def across(value):
    return lax.ppermute(value, "ctx", [(i, (i + 4) % 8) for i in range(8)])


def along(value, step):
    return lax.ppermute(value, "ctx", [(a * 4 + b, a * 4 + (b + step) % 4) for a in range(2) for b in range(4)])


def other_core(value):
    return lax.ppermute(value, "dp", [(i, i ^ 1) for i in range(16)])


def spot_of(place, far, step):
    half, row = place // 4, place % 4
    half = 1 - half if far else half
    return half * 4 + (row + step) % 4


def pack_kernel(place, qkv, out, up, down, vec, marks, near, far, qkv_s, out_s, up_s, down_s, vec_s, marks_s, semaphores):
    move = Mover(semaphores)
    arriving = [move.start(*p) for p in ((vec, vec_s), (marks, marks_s), (qkv, qkv_s), (out, out_s), (up, up_s), (down, down_s))]
    for copy in arriving:
        copy.wait()
    vec_row = jnp.concatenate([vec_s[...], jnp.zeros((1, EXTRA - 104), full)], axis=1)
    extra = jnp.concatenate([vec_row, marks_s[...].astype(full), jnp.zeros((6, EXTRA), full)], axis=0).astype(low)
    for is_far, parcel in ((1, far), (0, near)):
        for step in range(4):
            c = spot_of(place[0], is_far, step)
            cut = qkv_s[:, pl.ds(pl.multiple_of(c * QKV, 128), QKV)].astype(low)
            parts = [cut[:, (h * 3 + p) * HD : (h * 3 + p + 1) * HD] for p in range(3) for h in range(HEADS)]
            parcel[step, :, AT_QKV:AT_OUT] = jnp.concatenate(parts, axis=1)
            parcel[step, :, AT_UP : AT_UP + UP] = up_s[:, pl.ds(pl.multiple_of(c * UP, 128), UP)].astype(low)
            parcel[step, :, AT_OUT : AT_OUT + OUT] = out_s[:, pl.ds(pl.multiple_of(c * OUT, 128), OUT)].astype(low)
            parcel[step, :, AT_DOWN : AT_DOWN + UP] = down_s[:, pl.ds(pl.multiple_of(c * UP, 128), UP)].astype(low)
            parcel[step, :, AT_EXTRA:PARCEL] = extra


def regroup_kernel(near, far, *refs):
    for step in range(4):
        refs[step][0] = near[step]
        refs[step][1] = far[step]


def assemble_kernel(place, *refs):
    pieces, whole = refs[:4], refs[4]
    for step in range(4):
        for far in range(2):
            whole[pl.ds(spot_of(place[0], far, step), 1)] = pieces[step][far : far + 1]


def starts_kernel(marks, table, staged, semaphores):
    move = Mover(semaphores)
    whole = marks[...]
    start = jnp.zeros_like(whole)
    for k in range(1, 8):
        start = jnp.where(whole == k, jnp.sum((whole < k).astype(full), keepdims=True), start)
    row = lax.broadcasted_iota(jnp.int32, whole.shape, 0) * ROWS + lax.broadcasted_iota(jnp.int32, whole.shape, 1)
    positions = row.astype(full) - start
    slow = lax.broadcasted_iota(jnp.int32, (ROT // 2, 1), 0)
    frequency = jnp.zeros((ROT // 2, 1), full)
    for i, value in enumerate(FREQUENCIES):
        frequency = jnp.where(slow == i, value, frequency)
    turned = start.T
    for block in range(TP):
        rows = slice(block * ROWS, (block + 1) * ROWS)
        angles = positions[block : block + 1, :] * frequency
        cos_one = jnp.cos(angles).T
        sin_one = jnp.sin(angles).T
        start_one = jnp.broadcast_to(turned[:, block : block + 1], (ROWS, WIDTH - 2 * ROT))
        staged[rows, :] = jnp.concatenate([cos_one, cos_one, sin_one, sin_one, start_one], axis=1)
    move.send(staged, table)
    move.finish()


def norm_kernel(place, *refs):
    pieces, (whole, stored, staged, semaphores) = refs[:4], refs[4:]
    move = Mover(semaphores)
    arriving = [move.start(pieces[step], staged.at[step]) for step in range(4)]
    for step in range(4):
        arriving[step].wait()
        for far in range(2):
            spot = pl.multiple_of(spot_of(place[0], far, step) * ROWS, ROWS)
            normed, _ = normalise(staged[step, far * ROWS : (far + 1) * ROWS, :].astype(full))
            whole[pl.ds(spot, ROWS), :] = normed.astype(low)
    move.send(whole, stored)
    move.finish()


def angles_of(table):
    lane = lax.broadcasted_iota(jnp.int32, table.shape, 1)
    sine = pltpu.roll(table, WIDTH - ROT, 1)
    return tuple(jnp.where(lane < HD, t, pltpu.roll(t, HD, 1)) for t in (table, sine))


def turn(values, cosine, sine):
    lane = lax.broadcasted_iota(jnp.int32, values.shape, 1) % HD
    ahead = pltpu.roll(values, values.shape[1] - ROT // 2, 1)
    behind = pltpu.roll(values, ROT // 2, 1)
    turned = jnp.where(lane < ROT // 2, -ahead, behind)
    return jnp.where(lane < ROT, values * cosine + turned * sine, values)


def allowed_keys(block, starts):
    keys = (block + 1) * BLOCK
    row_index = block * BLOCK + lax.broadcasted_iota(jnp.int32, (BLOCK, keys), 0)
    key_index = lax.broadcasted_iota(jnp.int32, (BLOCK, keys), 1)
    return (key_index <= row_index) & (key_index >= starts.astype(jnp.int32))


def split_cores(core, rows):
    blocks = rows.reshape(rows.shape[0] // 128, 2, 64, rows.shape[1])
    mine = jnp.where(core == 0, blocks[:, 0], blocks[:, 1])
    others = jnp.where(core == 0, blocks[:, 1], blocks[:, 0])
    return mine.astype(low), others.astype(low)


def forward_kernel(
    place, normed, weights, table,
    attended_out, active_out, slope_out, scaled_out, qkv_out, table_out, bias_out, r0, r1, r2, r3,
    w_s, table_s, scaled, qkv, part_s, attended, active, slope, extra, flat, bias_s, semaphores,
):
    move = Mover(semaphores)
    step_rows = 256
    extra_arrives = move.start(weights.at[:, pl.ds(AT_EXTRA, EXTRA)], extra)
    table_arrives = move.start(table, table_s)
    arriving = [
        move.start(weights.at[pl.ds(r, step_rows), pl.ds(0, MIXED)], w_s.at[pl.ds(r, step_rows), pl.ds(0, MIXED)])
        for r in range(0, D, step_rows)
    ]
    extra_arrives.wait()
    owners = extra[...].astype(full).reshape(128, 8, EXTRA)[:, 0, :]
    for i in range(128):
        flat[:, i * 104 : (i + 1) * 104] = owners[i : i + 1, 0:104]
    bias_s[...] = flat[:, 7 * D : 8 * D] + flat[:, 12 * D : 13 * D]
    move.send(bias_s, bias_out)
    bias_up = flat[:, pl.ds(pl.multiple_of(8 * D + place[0] * UP, UP), UP)]
    bias_qkv = flat[:, pl.ds(pl.multiple_of(4 * D + place[0] * QKV, 128), QKV)]
    bias_qkv = [bias_qkv[:, (h * 3 + p) * HD : (h * 3 + p + 1) * HD] for p in range(3) for h in range(HEADS)]
    base = jnp.concatenate([bias_up] + bias_qkv, axis=1)
    table_arrives.wait()
    for r in range(0, D, 128):
        norms = [flat[:, n * D + r : n * D + r + 128] for n in range(4)]
        norms = jnp.concatenate(norms + [jnp.zeros((4, 128), full)], axis=0).T
        table_s[r : r + 128, AT_NORMS : AT_NORMS + 8] = norms
    for r in range(0, D, 128):
        if r % step_rows == 0:
            arriving[r // step_rows].wait()
        if r == D // 2:
            rest_arrives = move.start(weights.at[:, pl.ds(MIXED, OUT + UP)], w_s.at[:, pl.ds(MIXED, OUT + UP)])
        rows = pl.ds(r, 128)
        w = w_s[rows, 0:MIXED].astype(full)
        gain_one, shift_one, gain_two, shift_two = (table_s[rows, AT_NORMS + i : AT_NORMS + i + 1] for i in range(4))
        w_up, w_qkv = w[:, :UP], w[:, UP:]
        scaled[rows, :] = jnp.concatenate([gain_two * w_up, gain_one * w_qkv], axis=1).astype(low)
        base += jnp.concatenate(
            [jnp.sum(shift_two * w_up, axis=0, keepdims=True), jnp.sum(shift_one * w_qkv, axis=0, keepdims=True)], axis=1
        )
    move.send(scaled, scaled_out)

    def project(block, carry):
        rows = pl.ds(pl.multiple_of(block * BLOCK, BLOCK), BLOCK)
        projected = dot(normed[rows, :], scaled[:, AT_QKV:MIXED]) + base[:, AT_QKV:MIXED]
        cosine, sine = angles_of(table_s[rows, :])
        q = (turn(projected[:, 0:WIDTH], cosine, sine).astype(low) * (HD**-0.5)).astype(low)
        k = turn(projected[:, WIDTH : 2 * WIDTH], cosine, sine).astype(low)
        v = projected[:, 2 * WIDTH : 3 * WIDTH].astype(low)
        qkv[rows, :] = jnp.concatenate([q, k, v], axis=1)
        return carry

    lax.fori_loop(0, SEQ // BLOCK, project, 0)
    move.send(qkv, qkv_out)
    for block in range(SEQ // BLOCK):
        rows = pl.ds(block * BLOCK, BLOCK)
        allowed = allowed_keys(block, table_s[rows, AT_START : AT_START + 1])
        keys = (block + 1) * BLOCK
        for head in range(HEADS):
            at = head * HD
            q = qkv[rows, at : at + HD]
            k = qkv[0:keys, WIDTH + at : WIDTH + at + HD]
            v = qkv[0:keys, 2 * WIDTH + at : 2 * WIDTH + at + HD]
            scores = jnp.where(allowed, dot(q, k, NT), -1e30)
            most = jnp.max(scores, axis=-1, keepdims=True)
            expo = jnp.exp(scores - most)
            size = jnp.sum(expo, axis=-1, keepdims=True)
            attended[rows, at : at + HD] = (dot(expo.astype(low), v) * (1.0 / size)).astype(low)
            table_s[rows, AT_SIZE + head : AT_SIZE + head + 1] = most + jnp.log(size)
    move.send(attended, attended_out)
    move.send(table_s, table_out)
    half = UP // 2

    def feed(i, carry):
        rows = pl.ds(pl.multiple_of(i * BLOCK, BLOCK), BLOCK)
        for j in range(2):
            cols = slice(j * half, (j + 1) * half)
            hidden = dot(normed[rows, :], scaled[:, cols]) + base[:, cols]
            gate = 0.5 * (1.0 + lax.erf(hidden * (0.5**0.5)))
            active[rows, cols] = (hidden * gate).astype(low)
            inner = gate + hidden * jnp.exp(-0.5 * hidden * hidden) * (1.0 / math.sqrt(2.0 * math.pi))
            slope[rows, cols] = inner.astype(low)
        return carry

    lax.fori_loop(0, SEQ // BLOCK, feed, 0)
    move.send(active, active_out)
    move.send(slope, slope_out)
    rest_arrives.wait()
    for step, part in enumerate((r0, r1, r2, r3)):
        spots = [pl.ds(pl.multiple_of(spot_of(place[0], far, step) * ROWS, ROWS), ROWS) for far in range(2)]
        left = [jnp.concatenate([attended[spot, :], active[spot, :]], axis=1) for spot in spots]
        part_s[step] = dot(jnp.concatenate(left, axis=0), w_s[:, AT_OUT:AT_EXTRA], NT).astype(low)
        move.send(part_s.at[step], part)
    move.finish()


def backward_kernel(
    spots, upstream_total, attended_far, active_far, slope_far, dy0, dy1, dy2, dy3, normed, weights, table, qkv, scaled,
    keep, send, u0, u1, u2, u3,
    dy, w_s, normed_s, table_s, qkv_s, scaled_s, mixed, do_s, kept_s, sums, dq_s, dk_s, dv_s, keep_s, send_s, part_s, early,
    attended, active, slope, semaphores,
):
    move = Mover(semaphores)
    down_arrives = move.start(weights.at[:, pl.ds(AT_OUT, OUT + UP)], w_s.at[:, pl.ds(AT_OUT, OUT + UP)])
    dy_arrive = []

    def dy_start(step, piece):
        for far in range(2):
            spot = pl.multiple_of(spot_of(spots[0], far, step) * ROWS, ROWS)
            dy_arrive.append(move.start(piece.at[pl.ds(far * ROWS, ROWS)], dy.at[pl.ds(spot, ROWS)]))

    dy_start(0, dy0)
    held_arrive = [move.start(*p) for p in ((slope_far, slope), (attended_far, attended))]
    half = UP // 2
    dk_s[...] = jnp.zeros_like(dk_s)
    dv_s[...] = jnp.zeros_like(dv_s)
    early[...] = jnp.zeros_like(early)
    down_arrives.wait()
    for copy in held_arrive:
        copy.wait()
    for step, piece in ((1, dy1), (2, dy2), (3, dy3)):
        dy_start(step, piece)
    table_arrives = move.start(table, table_s)
    qkv_arrives = move.start(qkv, qkv_s)
    scaled_arrives = move.start(scaled, scaled_s)
    totals = [jnp.zeros((1, half), full)] * 2
    later = []
    for step in range(4):
        for copy in dy_arrive[2 * step : 2 * step + 2]:
            copy.wait()
        at = [pl.ds(pl.multiple_of(spot_of(spots[0], far, step) * ROWS, ROWS), ROWS) for far in range(2)]
        dy_now = jnp.concatenate([dy[rows, :] for rows in at], axis=0)
        for j in range(2):
            cols = slice(j * half, (j + 1) * half)
            d_active = dot(dy_now, w_s[:, AT_DOWN + j * half : AT_DOWN + (j + 1) * half])
            d_low = (d_active * jnp.concatenate([slope[rows, cols] for rows in at], axis=0).astype(full)).astype(low)
            for far in range(2):
                mixed[at[far], cols] = d_low[far * ROWS : (far + 1) * ROWS]
            totals[j] += jnp.sum(d_low.astype(full), axis=0, keepdims=True)
        d_out = dot(dy_now, w_s[:, AT_OUT : AT_OUT + OUT]).astype(low)
        for far in range(2):
            d_now = d_out[far * ROWS : (far + 1) * ROWS]
            do_s[at[far], :] = d_now
            product = d_now.astype(full) * attended[at[far], :].astype(full)
            for h in range(HEADS):
                kept_s[at[far], h : h + 1] = jnp.sum(product[:, h * HD : (h + 1) * HD], axis=-1, keepdims=True)
        if step == 0:
            later = [
                move.start(*p)
                for p in (
                    (normed, normed_s), (active_far, active),
                    (weights.at[:, pl.ds(0, MIXED)], w_s.at[:, pl.ds(0, MIXED)]),
                )
            ]
    hidden_total = jnp.concatenate(totals, axis=1)

    table_arrives.wait()
    qkv_arrives.wait()
    for block in range(SEQ // BLOCK):
        rows = pl.ds(block * BLOCK, BLOCK)
        allowed = allowed_keys(block, table_s[rows, AT_START : AT_START + 1])
        keys = (block + 1) * BLOCK
        for head in range(HEADS):
            at = head * HD
            lanes = pl.ds(at, HD)
            q = qkv_s[rows, at : at + HD]
            k = qkv_s[0:keys, WIDTH + at : WIDTH + at + HD]
            v = qkv_s[0:keys, 2 * WIDTH + at : 2 * WIDTH + at + HD]
            d_o = do_s[rows, lanes]
            scores = jnp.where(allowed, dot(q, k, NT), -1e30)
            weight = jnp.exp(scores - table_s[rows, AT_SIZE + head : AT_SIZE + head + 1])
            d_weight = dot(d_o, v, NT)
            d_scores = (weight * (d_weight - kept_s[rows, head : head + 1])).astype(low)
            dq_s[rows, lanes] = dot(d_scores, k) * (HD**-0.5)
            dk_s[0:keys, lanes] += dot(d_scores, q, TN)
            dv_s[0:keys, lanes] += dot(weight.astype(low), d_o, TN)
    total = jnp.zeros((1, QKV), full)
    for block in range(SEQ // BLOCK):
        rows = pl.ds(block * BLOCK, BLOCK)
        cosine, sine = angles_of(table_s[rows, :])
        sine = -sine
        back_low = jnp.concatenate(
            [turn(dq_s[rows, :], cosine, sine), turn(dk_s[rows, :], cosine, sine), dv_s[rows, :]], axis=1
        ).astype(low)
        mixed[rows, AT_QKV:MIXED] = back_low
        total += jnp.sum(back_low.astype(full), axis=0, keepdims=True)

    scaled_arrives.wait()
    for step, part in ((1, u1), (2, u2), (3, u3), (0, u0)):
        left = [mixed[pl.ds(pl.multiple_of(spot_of(spots[0], far, step) * ROWS, ROWS), ROWS), :] for far in range(2)]
        part_s[step] = dot(jnp.concatenate(left, axis=0), scaled_s[...], NT).astype(low)
        move.send(part_s.at[step], part)

    for copy in later:
        copy.wait()
    lane = lax.broadcasted_iota(jnp.int32, (BLOCK, 128), 1)
    mixed_total = jnp.concatenate([hidden_total, total], axis=1)
    for i in range(D // BLOCK):
        rows = pl.ds(i * BLOCK, BLOCK)
        places = pl.ds(i * (BLOCK // 128), BLOCK // 128)
        gain_one, shift_one, gain_two, shift_two = (table_s[rows, AT_NORMS + n : AT_NORMS + n + 1] for n in range(4))
        core_grad = dot(normed_s[:, rows], mixed[...], TN)
        w_mixed = w_s[rows, 0:MIXED].astype(full)
        gain_terms, shift_terms = w_mixed * core_grad, w_mixed * mixed_total
        found = [jnp.sum(t[:, c], axis=1, keepdims=True) for c in (slice(UP, MIXED), slice(0, UP)) for t in (gain_terms, shift_terms)]
        columns_now = jnp.zeros((BLOCK, 128), full)
        for n in range(4):
            columns_now = jnp.where(lane == n, found[n], columns_now)
        sums[rows, :] = columns_now
        grad_up = gain_two * core_grad[:, :UP] + shift_two * hidden_total
        grad_qkv = gain_one * core_grad[:, UP:] + shift_one * total
        grad_down = dot(dy[:, rows], active[...], TN)
        grad_out = dot(dy[:, rows], attended[...], TN)
        mine, others = split_cores(spots[1], jnp.concatenate([grad_up, grad_down, grad_out, grad_qkv], axis=1))
        keep_s[places, :, 0 : FEED + QKV] = mine
        send_s[places, :, 0 : FEED + QKV] = others
        for staged, target in ((send_s, send), (keep_s, keep)):
            done = (places, slice(None), pl.ds(0, FEED + QKV))
            move.send(staged.at[done], target.at[done])
    for r in range(0, D, 128):
        turned = sums[r : r + 128, :].T
        for n in range(4):
            early[:, n * D + r : n * D + r + 128] = turned[n : n + 1, :]
    bias_total = jnp.concatenate(
        [total[:, part * WIDTH + h * HD : part * WIDTH + (h + 1) * HD] for h in range(HEADS) for part in range(3)], axis=1
    )
    early[:, pl.ds(pl.multiple_of(4 * D + spots[0] * QKV, 128), QKV)] = bias_total
    early[:, 7 * D : 8 * D] = upstream_total[...]
    early[:, pl.ds(pl.multiple_of(8 * D + spots[0] * UP, UP), UP)] = hidden_total
    early[:, 12 * D : 13 * D] = upstream_total[...]
    for zl in range(8):
        parts = []
        for core in range(2):
            lines = []
            for c in range(TP):
                at = ((zl * 2 + core) * TP + c) * 104
                lines.append(jnp.concatenate([early[:, at : at + 104], jnp.zeros((1, EXTRA - 104), full)], axis=1))
                lines.append(jnp.zeros((7, EXTRA), full))
            parts.append(jnp.concatenate(lines, axis=0))
        keep_s[zl, :, FEED + QKV : PARCEL] = jnp.where(spots[1] == 0, parts[0], parts[1]).astype(low)
        send_s[zl, :, FEED + QKV : PARCEL] = jnp.where(spots[1] == 0, parts[1], parts[0]).astype(low)
    for staged, target in ((send_s, send), (keep_s, keep)):
        done = (slice(None), slice(None), pl.ds(FEED + QKV, EXTRA))
        move.send(staged.at[done], target.at[done])
    move.finish()


def update_kernel(grads, *refs):
    state, new = refs[:15], refs[15:30]

    def update(index, columns, gradient, rate, decay):
        results = adamw(*(state[3 * index + i][:, columns] for i in range(3)), gradient.astype(full), rate, decay)
        for i in range(3):
            new[3 * index + i][:, columns] = results[i]

    total = jnp.zeros((1, 104), full)
    for c in range(TP):
        at = FEED
        parts = [[grads[c, :, at + (p * HEADS + h) * HD : at + (p * HEADS + h + 1) * HD] for p in range(3)] for h in range(HEADS)]
        qkv = jnp.concatenate([part for head in parts for part in head], axis=1)
        update(0, slice(c * QKV, (c + 1) * QKV), qkv, 2.0 / math.sqrt(D), 0.1)
        update(1, slice(c * OUT, (c + 1) * OUT), grads[c, :, 2 * UP : FEED], 8.0 / math.sqrt(D), 0.1)
        update(2, slice(c * UP, (c + 1) * UP), grads[c, :, 0:UP], 2.0 / math.sqrt(D), 0.1)
        update(3, slice(c * UP, (c + 1) * UP), grads[c, :, UP : 2 * UP], 2.0 / math.sqrt(FF), 0.1)
        total += grads[c, :, FEED + QKV : FEED + QKV + 104].astype(full)[0:1, :]
    update(4, slice(0, 104), total, 0.5, 0.0)


def shift_rows(parts):
    return (parts[0], along(parts[1], 1), along(parts[2], 2), along(parts[3], -1))


def sum_rows(parts):
    total = sum(part.astype(full) for part in parts)
    return total[:ROWS], total[ROWS:].astype(low)


def local(
    inputs, segments, cotangent, qkv_weight, out_weight, up_weight, down_weight, vectors,
    qkv_first, qkv_second, out_first, out_second, up_first, up_second, down_first, down_second, vec_first, vec_second,
):
    place = lax.axis_index("ctx")
    rank = lax.axis_index("dp")
    place_one = place.reshape(1).astype(jnp.int32)
    core = lax.rem(rank, 2)
    spots = jnp.stack([place, core]).astype(jnp.int32)
    tokens = inputs[0]
    upstream = cotangent[0]

    quarter, piece = ((4, 8, PARCEL), low), ((2, 8, PARCEL), low)
    near, far = call(
        pack_kernel, "pack", [(quarter, VMEM)] * 2,
        [(place_one, SMEM)] + [(o, FAR) for o in (qkv_weight, out_weight, up_weight, down_weight, vectors.reshape(1, 104), segments)],
        scratch=[((8, n), full) for n in (3 * D, D, FF, FF)] + [((1, 104), full), ((1, ROWS), jnp.int32)], copies=6,
    )
    far, later_tokens = lax.optimization_barrier((across(far), tokens))
    far_tokens = across(later_tokens)
    sends = call(regroup_kernel, "regroup", [(piece, VMEM)] * 4, [(near, VMEM), (far, VMEM)])
    pieces = (sends[0], along(sends[3], -1), along(sends[2], 2), along(sends[1], 1))
    pieces, far_tokens = lax.optimization_barrier((pieces, far_tokens))
    (parcel,) = call(
        assemble_kernel, "assemble", [(((TP, 8, PARCEL), low), VMEM)], [(place_one, SMEM)] + [(o, VMEM) for o in pieces]
    )

    def rows_of(value, far_value):
        pair = jnp.concatenate([value, far_value], axis=0)
        return (pair, along(pair, -1), along(pair, 2), along(pair, 1))

    x_pieces = rows_of(tokens, far_tokens)
    far_upstream = across(upstream)
    marks = parcel[:, 1, AT_EXTRA:PARCEL].astype(full)
    (table,) = call(
        starts_kernel, "starts", [(((SEQ, WIDTH), full), FAR)], [(marks, VMEM)], scratch=[((SEQ, WIDTH), full)], copies=1
    )
    x_pieces, upstream, far_upstream, table = lax.optimization_barrier((x_pieces, upstream, far_upstream, table))
    dy_pieces = rows_of(upstream, far_upstream)
    weights = lax.all_gather(parcel.reshape(64, PARCEL), "dp", axis=0, tiled=True)

    square = ((SEQ, D), low)
    normed, normed_far = call(
        norm_kernel, "norm", [(square, VMEM), (square, FAR)], [(place_one, SMEM)] + [(o, FAR) for o in x_pieces],
        scratch=[((4, 2 * ROWS, D), low)], copies=5,
    )
    weights, normed, table = lax.optimization_barrier((weights, normed, table))
    pairs = ((2 * ROWS, D), low)
    head_rows, table_type, scaled_type, qkv_type, hidden_type = ((SEQ, WIDTH), low), ((SEQ, WIDTH), full), ((D, MIXED), low), ((SEQ, QKV), low), ((SEQ, UP), low)
    attended, active, slope, scaled, qkv, table, bias_out, *r_parts = call(
        forward_kernel, "forward",
        [(o, FAR) for o in (head_rows, hidden_type, hidden_type, scaled_type, qkv_type, table_type, ((1, D), full))] + [(pairs, FAR)] * 4,
        [(place_one, SMEM), (normed, VMEM), (weights, FAR), (table, FAR)],
        scratch=[
            ((D, AT_EXTRA), low), table_type, scaled_type, qkv_type, ((4, 2 * ROWS, D), low), head_rows, hidden_type, hidden_type,
            ((D, EXTRA), low), ((1, 13 * D), full), ((1, D), full),
        ],
        copies=18,
    )
    r_parts = shift_rows(r_parts)

    attended, dy_pieces = lax.optimization_barrier((attended, dy_pieces))
    upstream_total = jnp.sum(upstream.astype(full), axis=0, keepdims=True)
    parcel_type, kept_type = ((8, 64, PARCEL), low), ((SEQ, WIDTH), full)
    keep, send, *u_parts = call(
        backward_kernel, "backward",
        [(parcel_type, FAR)] * 2 + [(pairs, FAR)] * 4,
        [(spots, SMEM), (upstream_total, VMEM)]
        + [(o, FAR) for o in (attended, active, slope) + dy_pieces + (normed_far, weights, table, qkv, scaled)],
        scratch=[
            square, ((D, AT_EXTRA), low), square, table_type, qkv_type, scaled_type,
            ((SEQ, MIXED), low), head_rows, kept_type, kept_type, kept_type, kept_type, kept_type,
            parcel_type, parcel_type, ((4, 2 * ROWS, D), low), ((1, 13 * D), full),
            head_rows, hidden_type, hidden_type,
        ],
        copies=32,
    )
    keep, send, r_parts = lax.optimization_barrier((keep, send, r_parts))
    u_parts = shift_rows(u_parts)
    grads = (keep.astype(full) + other_core(send).astype(full)).astype(low)
    result, result_far = sum_rows(r_parts)
    grads, result_far = lax.optimization_barrier((grads, result_far))
    lanes = [[(zl * 2 + k) for zl in range(8)] for k in range(2)]
    grads = lax.all_to_all(grads, "dp", 0, 0, axis_index_groups=lanes, tiled=True)
    d_own, d_far = sum_rows(u_parts)
    grads, d_far, result_far = lax.optimization_barrier((grads, d_far, across(result_far)))
    grads = jnp.sum(grads.astype(full), axis=0).astype(low).reshape(TP, 8, PARCEL)
    own_grads = lax.all_to_all(grads, "ctx", 0, 0, tiled=True)
    d_own = d_own + across(d_far).astype(full)
    result = result + result_far.astype(full)

    outputs = tokens.astype(full) + result + bias_out
    own, rate = normalise(tokens.astype(full))
    d_tokens = rate * (
        d_own - jnp.mean(d_own, axis=-1, keepdims=True) - own * jnp.mean(d_own * own, axis=-1, keepdims=True)
    )
    input_grad = upstream.astype(full) + d_tokens

    outputs, input_grad, own_grads = lax.optimization_barrier((outputs.astype(low), input_grad, own_grads))
    state = (
        (qkv_weight, qkv_first, qkv_second), (out_weight, out_first, out_second), (up_weight, up_first, up_second),
        (down_weight, down_first, down_second), tuple(v.reshape(1, 104) for v in (vectors, vec_first, vec_second)),
    )
    state = [array for triple in state for array in triple]
    new = call(
        update_kernel, "update", [((o.shape, full), NEAR) for o in state], [(own_grads, VMEM)] + [(o, VMEM) for o in state],
    )
    return (outputs[None], input_grad[None]) + tuple(new[:12]) + tuple(v.reshape(104) for v in new[12:])


def solution(mesh):
    tokens = P("dp", "ctx", None)
    matrix = P(("dp", "ctx"), None)
    vector = P(("dp", "ctx"))
    return jax.shard_map(
        local,
        mesh=mesh,
        in_specs=(tokens, P("dp", "ctx"), tokens) + (matrix,) * 4 + (vector,) + (matrix,) * 8 + (vector,) * 2,
        out_specs=(tokens, tokens) + (matrix,) * 12 + (vector,) * 3,
        check_vma=False,
    )
```

```python
import math

import jax
import jax.numpy as jnp
import numpy as np
from jax import lax
from jax.experimental import pallas as pl
from jax.experimental.pallas import tpu as pltpu
from jax.sharding import PartitionSpec as P

D = 1024
H = 16
FF = 4096
HD = 64
ROT = 16
STEP = 10
SEQ = 1024
TP = 8
ROWS = SEQ // TP
HEADS = H // TP
WIDTH = HEADS * HD
QKV = 3 * D // TP
OUT = D // TP
UP = FF // TP
EXTRA = 128
MIXED = UP + QKV
FEED = 2 * UP + OUT
REST = QKV + EXTRA
BLOCK = 256

beta_one = 0.9
beta_two = 0.95
epsilon = 1e-08
norm_epsilon = 1e-05
FREQUENCIES = [float(f) for f in 10000.0 ** (-np.arange(ROT // 2, dtype=np.float32) * np.float32(2.0) / np.float32(ROT))]
low = jnp.bfloat16
full = jnp.float32

AT_UP = 0
AT_QKV = UP
AT_OUT = UP + QKV
AT_DOWN = AT_OUT + OUT
AT_EXTRA = AT_DOWN + UP
PARCEL = AT_EXTRA + EXTRA
AT_START = 2 * ROT
AT_SIZE = AT_START + 1
AT_NORMS = AT_SIZE + HEADS

NT = ((1,), (1,))
TN = ((0,), (0,))
VMEM = pl.BlockSpec(memory_space=pltpu.VMEM)
SMEM = pl.BlockSpec(memory_space=pltpu.SMEM)


def dot(a, b, dims=((1,), (0,))):
    return lax.dot_general(a, b, (dims, ((), ())), preferred_element_type=full)


FAR = pl.BlockSpec(memory_space=pltpu.HBM)
NEAR = pl.BlockSpec(memory_space=pltpu.VMEM)


def call(kernel, name, results, operands, scratch=(), copies=0, limit=40):
    spaces = {id(VMEM): pltpu.VMEM, id(FAR): pltpu.HBM, id(NEAR): jax.ShapeDtypeStruct}

    def held(operand, spec):
        return operand if spec is SMEM else pltpu.with_memory_space_constraint(operand, spaces[id(spec)])

    return pl.pallas_call(
        kernel,
        out_shape=tuple(spaces[id(spec)](*s) for s, spec in results),
        in_specs=[spec for _, spec in operands],
        out_specs=tuple(spec for _, spec in results),
        scratch_shapes=[pltpu.VMEM(*s) for s in scratch] + [pltpu.SemaphoreType.DMA((copies,))] * (copies > 0),
        compiler_params=pltpu.CompilerParams(vmem_limit_bytes=limit * 2**20),
        cost_estimate=pl.CostEstimate(flops=1024, bytes_accessed=1024, transcendentals=0),
        name=name,
    )(*(held(*o) for o in operands))


class Mover:
    def __init__(self, semaphores):
        self.semaphores, self.used, self.leaving = semaphores, 0, []

    def start(self, source, target):
        copy = pltpu.make_async_copy(source, target, self.semaphores.at[self.used])
        self.used += 1
        copy.start()
        return copy

    def send(self, source, target):
        self.leaving.append(self.start(source, target))

    def finish(self):
        for copy in self.leaving:
            copy.wait()


def adamw(weight, moment_one, moment_two, gradient, step_rate, decay_rate):
    moment_one = beta_one * moment_one + (1.0 - beta_one) * gradient
    moment_two = beta_two * moment_two + (1.0 - beta_two) * gradient * gradient
    fix_one = 1.0 - beta_one**STEP
    fix_two = 1.0 - beta_two**STEP
    update = moment_one / fix_one / (jnp.sqrt(moment_two / fix_two) + epsilon)
    weight = weight - step_rate * (update + decay_rate * weight)
    return (weight, moment_one, moment_two)


def normalise(values):
    center = values - jnp.mean(values, axis=-1, keepdims=True)
    spread = jnp.mean(center * center, axis=-1, keepdims=True)
    rate = lax.rsqrt(spread + norm_epsilon)
    return center * rate, rate


def across(value):
    return lax.ppermute(value, "ctx", [(i, (i + 4) % 8) for i in range(8)])


def along(value, step):
    return lax.ppermute(value, "ctx", [(a * 4 + b, a * 4 + (b + step) % 4) for a in range(2) for b in range(4)])


def other_core(value):
    return lax.ppermute(value, "dp", [(i, i ^ 1) for i in range(16)])


def spot_of(place, far, step):
    half, row = place // 4, place % 4
    half = 1 - half if far else half
    return half * 4 + (row + step) % 4


def pack_kernel(place, qkv, out, up, down, vec, marks, near, far, qkv_s, out_s, up_s, down_s, vec_s, marks_s, semaphores):
    move = Mover(semaphores)
    arriving = [move.start(*p) for p in ((vec, vec_s), (marks, marks_s), (qkv, qkv_s), (out, out_s), (up, up_s), (down, down_s))]
    for copy in arriving:
        copy.wait()
    vec_row = jnp.concatenate([vec_s[...], jnp.zeros((1, EXTRA - 104), full)], axis=1)
    extra = jnp.concatenate([vec_row, marks_s[...].astype(full), jnp.zeros((6, EXTRA), full)], axis=0).astype(low)
    for is_far, parcel in ((1, far), (0, near)):
        for step in range(4):
            c = spot_of(place[0], is_far, step)
            cut = qkv_s[:, pl.ds(pl.multiple_of(c * QKV, 128), QKV)].astype(low)
            parts = [cut[:, (h * 3 + p) * HD : (h * 3 + p + 1) * HD] for p in range(3) for h in range(HEADS)]
            parcel[step, :, AT_QKV:AT_OUT] = jnp.concatenate(parts, axis=1)
            parcel[step, :, AT_UP : AT_UP + UP] = up_s[:, pl.ds(pl.multiple_of(c * UP, 128), UP)].astype(low)
            parcel[step, :, AT_OUT : AT_OUT + OUT] = out_s[:, pl.ds(pl.multiple_of(c * OUT, 128), OUT)].astype(low)
            parcel[step, :, AT_DOWN : AT_DOWN + UP] = down_s[:, pl.ds(pl.multiple_of(c * UP, 128), UP)].astype(low)
            parcel[step, :, AT_EXTRA:PARCEL] = extra


def regroup_kernel(near, far, *refs):
    for step in range(4):
        refs[step][0] = near[step]
        refs[step][1] = far[step]


def assemble_kernel(place, *refs):
    pieces, whole = refs[:4], refs[4]
    for step in range(4):
        for far in range(2):
            whole[pl.ds(spot_of(place[0], far, step), 1)] = pieces[step][far : far + 1]


def starts_kernel(marks, table, staged, semaphores):
    move = Mover(semaphores)
    whole = marks[...]
    start = jnp.zeros_like(whole)
    for k in range(1, 8):
        start = jnp.where(whole == k, jnp.sum((whole < k).astype(full), keepdims=True), start)
    row = lax.broadcasted_iota(jnp.int32, whole.shape, 0) * ROWS + lax.broadcasted_iota(jnp.int32, whole.shape, 1)
    positions = row.astype(full) - start
    slow = lax.broadcasted_iota(jnp.int32, (ROT // 2, 1), 0)
    frequency = jnp.zeros((ROT // 2, 1), full)
    for i, value in enumerate(FREQUENCIES):
        frequency = jnp.where(slow == i, value, frequency)
    turned = start.T
    for block in range(TP):
        rows = slice(block * ROWS, (block + 1) * ROWS)
        angles = positions[block : block + 1, :] * frequency
        cos_one = jnp.cos(angles).T
        sin_one = jnp.sin(angles).T
        start_one = jnp.broadcast_to(turned[:, block : block + 1], (ROWS, WIDTH - 2 * ROT))
        staged[rows, :] = jnp.concatenate([cos_one, cos_one, sin_one, sin_one, start_one], axis=1)
    move.send(staged, table)
    move.finish()


def norm_kernel(place, *refs):
    pieces, (whole, stored, staged, semaphores) = refs[:4], refs[4:]
    move = Mover(semaphores)
    arriving = [move.start(pieces[step], staged.at[step]) for step in range(4)]
    for step in range(4):
        arriving[step].wait()
        for far in range(2):
            spot = pl.multiple_of(spot_of(place[0], far, step) * ROWS, ROWS)
            normed, _ = normalise(staged[step, far * ROWS : (far + 1) * ROWS, :].astype(full))
            whole[pl.ds(spot, ROWS), :] = normed.astype(low)
    move.send(whole, stored)
    move.finish()


def angles_of(table):
    lane = lax.broadcasted_iota(jnp.int32, table.shape, 1)
    sine = pltpu.roll(table, WIDTH - ROT, 1)
    return tuple(jnp.where(lane < HD, t, pltpu.roll(t, HD, 1)) for t in (table, sine))


def turn(values, cosine, sine):
    lane = lax.broadcasted_iota(jnp.int32, values.shape, 1) % HD
    ahead = pltpu.roll(values, values.shape[1] - ROT // 2, 1)
    behind = pltpu.roll(values, ROT // 2, 1)
    turned = jnp.where(lane < ROT // 2, -ahead, behind)
    return jnp.where(lane < ROT, values * cosine + turned * sine, values)


def masked_scores(q, k, starts, block):
    before = block * BLOCK
    first = starts.astype(jnp.int32)
    key = lax.broadcasted_iota(jnp.int32, (BLOCK, BLOCK), 1)
    row = lax.broadcasted_iota(jnp.int32, (BLOCK, BLOCK), 0)
    near = jnp.where((key <= row) & (key + before >= first), dot(q, k[before:], NT), -1e30)
    if block == 0:
        return near
    key = lax.broadcasted_iota(jnp.int32, (BLOCK, before), 1)
    return jnp.concatenate([jnp.where(key >= first, dot(q, k[:before], NT), -1e30), near], axis=1)


def split_cores(core, rows):
    blocks = rows.reshape(rows.shape[0] // 128, 2, 64, rows.shape[1])
    mine = jnp.where(core == 0, blocks[:, 0], blocks[:, 1])
    others = jnp.where(core == 0, blocks[:, 1], blocks[:, 0])
    return mine.astype(low), others.astype(low)


def forward_kernel(
    place, normed, weights, table,
    attended_out, active_out, slope_out, scaled_out, qkv_out, table_out, bias_out, r0, r1, r2, r3,
    w_s, table_s, scaled, qkv, part_s, attended, active, slope, extra, flat, bias_s, semaphores,
):
    move = Mover(semaphores)
    step_rows = 256
    extra_arrives = move.start(weights.at[:, pl.ds(AT_EXTRA, EXTRA)], extra)
    table_arrives = move.start(table, table_s)
    arriving = [
        move.start(weights.at[pl.ds(r, step_rows), pl.ds(0, MIXED)], w_s.at[pl.ds(r, step_rows), pl.ds(0, MIXED)])
        for r in range(0, D, step_rows)
    ]
    extra_arrives.wait()
    owners = extra[...].astype(full).reshape(128, 8, EXTRA)[:, 0, :]
    for i in range(128):
        flat[:, i * 104 : (i + 1) * 104] = owners[i : i + 1, 0:104]
    bias_s[...] = flat[:, 7 * D : 8 * D] + flat[:, 12 * D : 13 * D]
    move.send(bias_s, bias_out)
    bias_up = flat[:, pl.ds(pl.multiple_of(8 * D + place[0] * UP, UP), UP)]
    bias_qkv = flat[:, pl.ds(pl.multiple_of(4 * D + place[0] * QKV, 128), QKV)]
    bias_qkv = [bias_qkv[:, (h * 3 + p) * HD : (h * 3 + p + 1) * HD] for p in range(3) for h in range(HEADS)]
    base = jnp.concatenate([bias_up] + bias_qkv, axis=1)
    table_arrives.wait()
    for r in range(0, D, 128):
        norms = [flat[:, n * D + r : n * D + r + 128] for n in range(4)]
        norms = jnp.concatenate(norms + [jnp.zeros((4, 128), full)], axis=0).T
        table_s[r : r + 128, AT_NORMS : AT_NORMS + 8] = norms
    for r in range(0, D, 128):
        if r % step_rows == 0:
            arriving[r // step_rows].wait()
        if r == D // 2:
            rest_arrives = move.start(weights.at[:, pl.ds(MIXED, OUT + UP)], w_s.at[:, pl.ds(MIXED, OUT + UP)])
        rows = pl.ds(r, 128)
        w = w_s[rows, 0:MIXED].astype(full)
        gain_one, shift_one, gain_two, shift_two = (table_s[rows, AT_NORMS + i : AT_NORMS + i + 1] for i in range(4))
        w_up, w_qkv = w[:, :UP], w[:, UP:]
        scaled[rows, :] = jnp.concatenate([gain_two * w_up, gain_one * w_qkv], axis=1).astype(low)
        base += jnp.concatenate(
            [jnp.sum(shift_two * w_up, axis=0, keepdims=True), jnp.sum(shift_one * w_qkv, axis=0, keepdims=True)], axis=1
        )
    move.send(scaled, scaled_out)

    for block in range(SEQ // BLOCK):
        rows = pl.ds(block * BLOCK, BLOCK)
        projected = dot(normed[rows, :], scaled[:, AT_QKV:MIXED]) + base[:, AT_QKV:MIXED]
        cosine, sine = angles_of(table_s[rows, :])
        q = (turn(projected[:, 0:WIDTH], cosine, sine).astype(low) * (HD**-0.5)).astype(low)
        k = turn(projected[:, WIDTH : 2 * WIDTH], cosine, sine).astype(low)
        v = projected[:, 2 * WIDTH : 3 * WIDTH].astype(low)
        qkv[rows, :] = jnp.concatenate([q, k, v], axis=1)
        starts = table_s[rows, AT_START : AT_START + 1]
        keys = (block + 1) * BLOCK
        both = []
        half = UP // 2
        for j in range(2):
            cols = slice(j * half, (j + 1) * half)
            hidden = dot(normed[rows, :], scaled[:, cols]) + base[:, cols]
            gate = 0.5 * (1.0 + lax.erf(hidden * (0.5**0.5)))
            active[rows, cols] = (hidden * gate).astype(low)
            inner = gate + hidden * jnp.exp(-0.5 * hidden * hidden) * (1.0 / math.sqrt(2.0 * math.pi))
            slope[rows, cols] = inner.astype(low)
        for head in range(HEADS):
            at = head * HD
            both.append(masked_scores(qkv[rows, at : at + HD], qkv[0:keys, WIDTH + at : WIDTH + at + HD], starts, block))
        for head in range(HEADS):
            at = head * HD
            v = qkv[0:keys, 2 * WIDTH + at : 2 * WIDTH + at + HD]
            scores = both[head]
            most = jnp.max(scores, axis=-1, keepdims=True)
            expo = jnp.exp(scores - most)
            size = jnp.sum(expo, axis=-1, keepdims=True)
            attended[rows, at : at + HD] = (dot(expo.astype(low), v) * (1.0 / size)).astype(low)
            table_s[rows, AT_SIZE + head : AT_SIZE + head + 1] = most + jnp.log(size)
    move.send(qkv, qkv_out)
    move.send(attended, attended_out)
    move.send(table_s, table_out)
    move.send(active, active_out)
    move.send(slope, slope_out)
    rest_arrives.wait()
    for step, part in enumerate((r0, r1, r2, r3)):
        spots = [pl.ds(pl.multiple_of(spot_of(place[0], far, step) * ROWS, ROWS), ROWS) for far in range(2)]
        left = [jnp.concatenate([attended[spot, :], active[spot, :]], axis=1) for spot in spots]
        part_s[step] = dot(jnp.concatenate(left, axis=0), w_s[:, AT_OUT:AT_EXTRA], NT).astype(low)
        move.send(part_s.at[step], part)
    move.finish()


def backward_kernel(
    spots, upstream_total, attended_far, active_far, slope_far, dy0, dy1, dy2, dy3, normed, weights, table, qkv, scaled,
    keep, send, u0, u1, u2, u3,
    dy, w_s, normed_s, table_s, qkv_s, scaled_s, mixed, do_s, kept_s, sums, dq_s, dk_s, dv_s, keep_s, send_s, part_s, early,
    attended, active, slope, semaphores,
):
    move = Mover(semaphores)
    down_arrives = move.start(weights.at[:, pl.ds(AT_OUT, OUT + UP)], w_s.at[:, pl.ds(AT_OUT, OUT + UP)])
    dy_arrive = []

    def dy_start(step, piece):
        for far in range(2):
            spot = pl.multiple_of(spot_of(spots[0], far, step) * ROWS, ROWS)
            dy_arrive.append(move.start(piece.at[pl.ds(far * ROWS, ROWS)], dy.at[pl.ds(spot, ROWS)]))

    dy_start(0, dy0)
    held_arrive = [move.start(*p) for p in ((slope_far, slope), (attended_far, attended))]
    half = UP // 2
    dk_s[...] = jnp.zeros_like(dk_s)
    dv_s[...] = jnp.zeros_like(dv_s)
    early[...] = jnp.zeros_like(early)
    down_arrives.wait()
    for copy in held_arrive:
        copy.wait()
    for step, piece in ((1, dy1), (2, dy2), (3, dy3)):
        dy_start(step, piece)
    table_arrives = move.start(table, table_s)
    qkv_arrives = move.start(qkv, qkv_s)
    scaled_arrives = move.start(scaled, scaled_s)
    totals = [jnp.zeros((1, half), full)] * 2
    later = []
    for step in range(4):
        for copy in dy_arrive[2 * step : 2 * step + 2]:
            copy.wait()
        at = [pl.ds(pl.multiple_of(spot_of(spots[0], far, step) * ROWS, ROWS), ROWS) for far in range(2)]
        dy_now = jnp.concatenate([dy[rows, :] for rows in at], axis=0)
        for j in range(2):
            cols = slice(j * half, (j + 1) * half)
            d_active = dot(dy_now, w_s[:, AT_DOWN + j * half : AT_DOWN + (j + 1) * half])
            d_low = (d_active * jnp.concatenate([slope[rows, cols] for rows in at], axis=0).astype(full)).astype(low)
            for far in range(2):
                mixed[at[far], cols] = d_low[far * ROWS : (far + 1) * ROWS]
            totals[j] += jnp.sum(d_low.astype(full), axis=0, keepdims=True)
        d_out = dot(dy_now, w_s[:, AT_OUT : AT_OUT + OUT]).astype(low)
        for far in range(2):
            d_now = d_out[far * ROWS : (far + 1) * ROWS]
            do_s[at[far], :] = d_now
            product = d_now.astype(full) * attended[at[far], :].astype(full)
            for h in range(HEADS):
                kept_s[at[far], h : h + 1] = jnp.sum(product[:, h * HD : (h + 1) * HD], axis=-1, keepdims=True)
        if step == 0:
            later = [
                move.start(*p)
                for p in (
                    (normed, normed_s), (active_far, active),
                    (weights.at[:, pl.ds(0, MIXED)], w_s.at[:, pl.ds(0, MIXED)]),
                )
            ]
    hidden_total = jnp.concatenate(totals, axis=1)

    table_arrives.wait()
    qkv_arrives.wait()
    for copy in later:
        copy.wait()
    lane = lax.broadcasted_iota(jnp.int32, (BLOCK, 128), 1)
    for block in range(SEQ // BLOCK):
        rows = pl.ds(block * BLOCK, BLOCK)
        starts = table_s[rows, AT_START : AT_START + 1]
        keys = (block + 1) * BLOCK
        places = pl.ds(block * (BLOCK // 128), BLOCK // 128)
        gain_two, shift_two = (table_s[rows, AT_NORMS + n : AT_NORMS + n + 1] for n in (2, 3))
        core_up = dot(normed_s[:, rows], mixed[:, 0:UP], TN)
        w_up = w_s[rows, 0:UP].astype(full)
        found = [jnp.sum(t, axis=1, keepdims=True) for t in (w_up * core_up, w_up * hidden_total)]
        sums[rows, :] = jnp.where(lane == 2, found[0], found[1])
        grad_up = gain_two * core_up + shift_two * hidden_total
        grad_down = dot(dy[:, rows], active[...], TN)
        grad_out = dot(dy[:, rows], attended[...], TN)
        mine, others = split_cores(spots[1], jnp.concatenate([grad_up, grad_down, grad_out], axis=1))
        keep_s[places, :, 0:FEED] = mine
        send_s[places, :, 0:FEED] = others
        for head in range(HEADS):
            at = head * HD
            lanes = pl.ds(at, HD)
            q = qkv_s[rows, at : at + HD]
            k = qkv_s[0:keys, WIDTH + at : WIDTH + at + HD]
            v = qkv_s[0:keys, 2 * WIDTH + at : 2 * WIDTH + at + HD]
            d_o = do_s[rows, lanes]
            scores = masked_scores(q, k, starts, block)
            weight = jnp.exp(scores - table_s[rows, AT_SIZE + head : AT_SIZE + head + 1])
            d_weight = dot(d_o, v, NT)
            d_scores = (weight * (d_weight - kept_s[rows, head : head + 1])).astype(low)
            dq_s[rows, lanes] = dot(d_scores, k) * (HD**-0.5)
            dk_s[0:keys, lanes] += dot(d_scores, q, TN)
            dv_s[0:keys, lanes] += dot(weight.astype(low), d_o, TN)
    total = jnp.zeros((1, QKV), full)
    for block in range(SEQ // BLOCK):
        rows = pl.ds(block * BLOCK, BLOCK)
        cosine, sine = angles_of(table_s[rows, :])
        sine = -sine
        back_low = jnp.concatenate(
            [turn(dq_s[rows, :], cosine, sine), turn(dk_s[rows, :], cosine, sine), dv_s[rows, :]], axis=1
        ).astype(low)
        mixed[rows, AT_QKV:MIXED] = back_low
        total += jnp.sum(back_low.astype(full), axis=0, keepdims=True)

    scaled_arrives.wait()
    for step, part in ((1, u1), (2, u2), (3, u3), (0, u0)):
        left = [mixed[pl.ds(pl.multiple_of(spot_of(spots[0], far, step) * ROWS, ROWS), ROWS), :] for far in range(2)]
        part_s[step] = dot(jnp.concatenate(left, axis=0), scaled_s[...], NT).astype(low)
        move.send(part_s.at[step], part)

    for i in range(D // BLOCK):
        rows = pl.ds(i * BLOCK, BLOCK)
        places = pl.ds(i * (BLOCK // 128), BLOCK // 128)
        gain_one, shift_one = (table_s[rows, AT_NORMS + n : AT_NORMS + n + 1] for n in (0, 1))
        core_qkv = dot(normed_s[:, rows], mixed[:, UP:MIXED], TN)
        w_qkv = w_s[rows, UP:MIXED].astype(full)
        found = [jnp.sum(t, axis=1, keepdims=True) for t in (w_qkv * core_qkv, w_qkv * total)]
        sums[rows, :] = jnp.where(lane == 0, found[0], jnp.where(lane == 1, found[1], sums[rows, :]))
        mine, others = split_cores(spots[1], gain_one * core_qkv + shift_one * total)
        keep_s[places, :, FEED : FEED + QKV] = mine
        send_s[places, :, FEED : FEED + QKV] = others
        for staged, target in ((send_s, send), (keep_s, keep)):
            done = (places, slice(None), pl.ds(0, FEED + QKV))
            move.send(staged.at[done], target.at[done])
    for r in range(0, D, 128):
        turned = sums[r : r + 128, :].T
        for n in range(4):
            early[:, n * D + r : n * D + r + 128] = turned[n : n + 1, :]
    bias_total = jnp.concatenate(
        [total[:, part * WIDTH + h * HD : part * WIDTH + (h + 1) * HD] for h in range(HEADS) for part in range(3)], axis=1
    )
    early[:, pl.ds(pl.multiple_of(4 * D + spots[0] * QKV, 128), QKV)] = bias_total
    early[:, 7 * D : 8 * D] = upstream_total[...]
    early[:, pl.ds(pl.multiple_of(8 * D + spots[0] * UP, UP), UP)] = hidden_total
    early[:, 12 * D : 13 * D] = upstream_total[...]
    for zl in range(8):
        parts = []
        for core in range(2):
            lines = []
            for c in range(TP):
                at = ((zl * 2 + core) * TP + c) * 104
                lines.append(jnp.concatenate([early[:, at : at + 104], jnp.zeros((1, EXTRA - 104), full)], axis=1))
                lines.append(jnp.zeros((7, EXTRA), full))
            parts.append(jnp.concatenate(lines, axis=0))
        keep_s[zl, :, FEED + QKV : PARCEL] = jnp.where(spots[1] == 0, parts[0], parts[1]).astype(low)
        send_s[zl, :, FEED + QKV : PARCEL] = jnp.where(spots[1] == 0, parts[1], parts[0]).astype(low)
    for staged, target in ((send_s, send), (keep_s, keep)):
        done = (slice(None), slice(None), pl.ds(FEED + QKV, EXTRA))
        move.send(staged.at[done], target.at[done])
    move.finish()


def update_kernel(grads, *refs):
    state, new = refs[:15], refs[15:30]

    def update(index, columns, gradient, rate, decay):
        results = adamw(*(state[3 * index + i][:, columns] for i in range(3)), gradient.astype(full), rate, decay)
        for i in range(3):
            new[3 * index + i][:, columns] = results[i]

    total = jnp.zeros((1, 104), full)
    for c in range(TP):
        at = FEED
        parts = [[grads[c, :, at + (p * HEADS + h) * HD : at + (p * HEADS + h + 1) * HD] for p in range(3)] for h in range(HEADS)]
        qkv = jnp.concatenate([part for head in parts for part in head], axis=1)
        update(0, slice(c * QKV, (c + 1) * QKV), qkv, 2.0 / math.sqrt(D), 0.1)
        update(1, slice(c * OUT, (c + 1) * OUT), grads[c, :, 2 * UP : FEED], 8.0 / math.sqrt(D), 0.1)
        update(2, slice(c * UP, (c + 1) * UP), grads[c, :, 0:UP], 2.0 / math.sqrt(D), 0.1)
        update(3, slice(c * UP, (c + 1) * UP), grads[c, :, UP : 2 * UP], 2.0 / math.sqrt(FF), 0.1)
        total += grads[c, :, FEED + QKV : FEED + QKV + 104].astype(full)[0:1, :]
    update(4, slice(0, 104), total, 0.5, 0.0)


def shift_rows(parts):
    return (parts[0], along(parts[1], 1), along(parts[2], 2), along(parts[3], -1))


def sum_rows(parts):
    total = sum(part.astype(full) for part in parts)
    return total[:ROWS], total[ROWS:].astype(low)


def local(
    inputs, segments, cotangent, qkv_weight, out_weight, up_weight, down_weight, vectors,
    qkv_first, qkv_second, out_first, out_second, up_first, up_second, down_first, down_second, vec_first, vec_second,
):
    place = lax.axis_index("ctx")
    rank = lax.axis_index("dp")
    place_one = place.reshape(1).astype(jnp.int32)
    core = lax.rem(rank, 2)
    spots = jnp.stack([place, core]).astype(jnp.int32)
    tokens = inputs[0]
    upstream = cotangent[0]

    quarter, piece = ((4, 8, PARCEL), low), ((2, 8, PARCEL), low)
    near, far = call(
        pack_kernel, "pack", [(quarter, VMEM)] * 2,
        [(place_one, SMEM)] + [(o, FAR) for o in (qkv_weight, out_weight, up_weight, down_weight, vectors.reshape(1, 104), segments)],
        scratch=[((8, n), full) for n in (3 * D, D, FF, FF)] + [((1, 104), full), ((1, ROWS), jnp.int32)], copies=6,
    )
    far, later_tokens = lax.optimization_barrier((across(far), tokens))
    far_tokens = across(later_tokens)
    sends = call(regroup_kernel, "regroup", [(piece, VMEM)] * 4, [(near, VMEM), (far, VMEM)])
    pieces = (sends[0], along(sends[3], -1), along(sends[2], 2), along(sends[1], 1))
    pieces, far_tokens = lax.optimization_barrier((pieces, far_tokens))
    (parcel,) = call(
        assemble_kernel, "assemble", [(((TP, 8, PARCEL), low), VMEM)], [(place_one, SMEM)] + [(o, VMEM) for o in pieces]
    )

    def rows_of(value, far_value):
        pair = jnp.concatenate([value, far_value], axis=0)
        return (pair, along(pair, -1), along(pair, 2), along(pair, 1))

    x_pieces = rows_of(tokens, far_tokens)
    far_upstream = across(upstream)
    marks = parcel[:, 1, AT_EXTRA:PARCEL].astype(full)
    (table,) = call(
        starts_kernel, "starts", [(((SEQ, WIDTH), full), FAR)], [(marks, VMEM)], scratch=[((SEQ, WIDTH), full)], copies=1
    )
    x_pieces, upstream, far_upstream, table = lax.optimization_barrier((x_pieces, upstream, far_upstream, table))
    dy_pieces = rows_of(upstream, far_upstream)
    weights = lax.all_gather(parcel.reshape(64, PARCEL), "dp", axis=0, tiled=True)

    square = ((SEQ, D), low)
    normed, normed_far = call(
        norm_kernel, "norm", [(square, VMEM), (square, FAR)], [(place_one, SMEM)] + [(o, FAR) for o in x_pieces],
        scratch=[((4, 2 * ROWS, D), low)], copies=5,
    )
    weights, normed, table = lax.optimization_barrier((weights, normed, table))
    pairs = ((2 * ROWS, D), low)
    head_rows, table_type, scaled_type, qkv_type, hidden_type = ((SEQ, WIDTH), low), ((SEQ, WIDTH), full), ((D, MIXED), low), ((SEQ, QKV), low), ((SEQ, UP), low)
    attended, active, slope, scaled, qkv, table, bias_out, *r_parts = call(
        forward_kernel, "forward",
        [(o, FAR) for o in (head_rows, hidden_type, hidden_type, scaled_type, qkv_type, table_type, ((1, D), full))] + [(pairs, FAR)] * 4,
        [(place_one, SMEM), (normed, VMEM), (weights, FAR), (table, FAR)],
        scratch=[
            ((D, AT_EXTRA), low), table_type, scaled_type, qkv_type, ((4, 2 * ROWS, D), low), head_rows, hidden_type, hidden_type,
            ((D, EXTRA), low), ((1, 13 * D), full), ((1, D), full),
        ],
        copies=18,
    )
    r_parts = shift_rows(r_parts)

    attended, dy_pieces = lax.optimization_barrier((attended, dy_pieces))
    upstream_total = jnp.sum(upstream.astype(full), axis=0, keepdims=True)
    parcel_type, kept_type = ((8, 64, PARCEL), low), ((SEQ, WIDTH), full)
    keep, send, *u_parts = call(
        backward_kernel, "backward",
        [(parcel_type, FAR)] * 2 + [(pairs, FAR)] * 4,
        [(spots, SMEM), (upstream_total, VMEM)]
        + [(o, FAR) for o in (attended, active, slope) + dy_pieces + (normed_far, weights, table, qkv, scaled)],
        scratch=[
            square, ((D, AT_EXTRA), low), square, table_type, qkv_type, scaled_type,
            ((SEQ, MIXED), low), head_rows, kept_type, kept_type, kept_type, kept_type, kept_type,
            parcel_type, parcel_type, ((4, 2 * ROWS, D), low), ((1, 13 * D), full),
            head_rows, hidden_type, hidden_type,
        ],
        copies=32,
    )
    keep, send, r_parts = lax.optimization_barrier((keep, send, r_parts))
    u_parts = shift_rows(u_parts)
    grads = (keep.astype(full) + other_core(send).astype(full)).astype(low)
    result, result_far = sum_rows(r_parts)
    grads, result_far = lax.optimization_barrier((grads, result_far))
    lanes = [[(zl * 2 + k) for zl in range(8)] for k in range(2)]
    grads = lax.all_to_all(grads, "dp", 0, 0, axis_index_groups=lanes, tiled=True)
    d_own, d_far = sum_rows(u_parts)
    grads, d_far, result_far = lax.optimization_barrier((grads, d_far, across(result_far)))
    grads = jnp.sum(grads.astype(full), axis=0).astype(low).reshape(TP, 8, PARCEL)
    own_grads = lax.all_to_all(grads, "ctx", 0, 0, tiled=True)
    d_own = d_own + across(d_far).astype(full)
    result = result + result_far.astype(full)

    outputs = tokens.astype(full) + result + bias_out
    own, rate = normalise(tokens.astype(full))
    d_tokens = rate * (
        d_own - jnp.mean(d_own, axis=-1, keepdims=True) - own * jnp.mean(d_own * own, axis=-1, keepdims=True)
    )
    input_grad = upstream.astype(full) + d_tokens

    outputs, input_grad, own_grads = lax.optimization_barrier((outputs.astype(low), input_grad, own_grads))
    state = (
        (qkv_weight, qkv_first, qkv_second), (out_weight, out_first, out_second), (up_weight, up_first, up_second),
        (down_weight, down_first, down_second), tuple(v.reshape(1, 104) for v in (vectors, vec_first, vec_second)),
    )
    state = [array for triple in state for array in triple]
    new = call(
        update_kernel, "update", [((o.shape, full), NEAR) for o in state], [(own_grads, VMEM)] + [(o, VMEM) for o in state],
    )
    return (outputs[None], input_grad[None]) + tuple(new[:12]) + tuple(v.reshape(104) for v in new[12:])


def solution(mesh):
    tokens = P("dp", "ctx", None)
    matrix = P(("dp", "ctx"), None)
    vector = P(("dp", "ctx"))
    return jax.shard_map(
        local,
        mesh=mesh,
        in_specs=(tokens, P("dp", "ctx"), tokens) + (matrix,) * 4 + (vector,) + (matrix,) * 8 + (vector,) * 2,
        out_specs=(tokens, tokens) + (matrix,) * 12 + (vector,) * 3,
        check_vma=False,
    )
```

```python
import math

import jax
import jax.numpy as jnp
import numpy as np
from jax import lax
from jax.experimental import pallas as pl
from jax.experimental.pallas import tpu as pltpu
from jax.sharding import PartitionSpec as P

D = 1024
H = 16
FF = 4096
HD = 64
ROT = 16
STEP = 10
SEQ = 1024
TP = 8
ROWS = SEQ // TP
HEADS = H // TP
WIDTH = HEADS * HD
QKV = 3 * D // TP
OUT = D // TP
UP = FF // TP
EXTRA = 128
MIXED = UP + QKV
FEED = 2 * UP + OUT
REST = QKV + EXTRA
BLOCK = 256

beta_one = 0.9
beta_two = 0.95
epsilon = 1e-08
norm_epsilon = 1e-05
FREQUENCIES = [float(f) for f in 10000.0 ** (-np.arange(ROT // 2, dtype=np.float32) * np.float32(2.0) / np.float32(ROT))]
low = jnp.bfloat16
full = jnp.float32

AT_UP = 0
AT_QKV = UP
AT_OUT = UP + QKV
AT_DOWN = AT_OUT + OUT
AT_EXTRA = AT_DOWN + UP
PARCEL = AT_EXTRA + EXTRA
AT_START = 2 * ROT
AT_SIZE = AT_START + 1
AT_NORMS = AT_SIZE + HEADS

NT = ((1,), (1,))
TN = ((0,), (0,))
VMEM = pl.BlockSpec(memory_space=pltpu.VMEM)
SMEM = pl.BlockSpec(memory_space=pltpu.SMEM)


def dot(a, b, dims=((1,), (0,))):
    return lax.dot_general(a, b, (dims, ((), ())), preferred_element_type=full)


FAR = pl.BlockSpec(memory_space=pltpu.HBM)
NEAR = pl.BlockSpec(memory_space=pltpu.VMEM)


def call(kernel, name, results, operands, scratch=(), copies=0, limit=40):
    spaces = {id(VMEM): pltpu.VMEM, id(FAR): pltpu.HBM, id(NEAR): jax.ShapeDtypeStruct}

    def held(operand, spec):
        return operand if spec is SMEM else pltpu.with_memory_space_constraint(operand, spaces[id(spec)])

    return pl.pallas_call(
        kernel,
        out_shape=tuple(spaces[id(spec)](*s) for s, spec in results),
        in_specs=[spec for _, spec in operands],
        out_specs=tuple(spec for _, spec in results),
        scratch_shapes=[pltpu.VMEM(*s) for s in scratch] + [pltpu.SemaphoreType.DMA((copies,))] * (copies > 0),
        compiler_params=pltpu.CompilerParams(vmem_limit_bytes=limit * 2**20),
        cost_estimate=pl.CostEstimate(flops=1024, bytes_accessed=1024, transcendentals=0),
        name=name,
    )(*(held(*o) for o in operands))


class Mover:
    def __init__(self, semaphores):
        self.semaphores, self.used, self.leaving = semaphores, 0, []

    def start(self, source, target):
        copy = pltpu.make_async_copy(source, target, self.semaphores.at[self.used])
        self.used += 1
        copy.start()
        return copy

    def send(self, source, target):
        self.leaving.append(self.start(source, target))

    def finish(self):
        for copy in self.leaving:
            copy.wait()


def adamw(weight, moment_one, moment_two, gradient, step_rate, decay_rate):
    moment_one = beta_one * moment_one + (1.0 - beta_one) * gradient
    moment_two = beta_two * moment_two + (1.0 - beta_two) * gradient * gradient
    fix_one = 1.0 - beta_one**STEP
    fix_two = 1.0 - beta_two**STEP
    update = moment_one / fix_one / (jnp.sqrt(moment_two / fix_two) + epsilon)
    weight = weight - step_rate * (update + decay_rate * weight)
    return (weight, moment_one, moment_two)


def normalise(values):
    center = values - jnp.mean(values, axis=-1, keepdims=True)
    spread = jnp.mean(center * center, axis=-1, keepdims=True)
    rate = lax.rsqrt(spread + norm_epsilon)
    return center * rate, rate


def across(value):
    return lax.ppermute(value, "ctx", [(i, (i + 4) % 8) for i in range(8)])


def along(value, step):
    return lax.ppermute(value, "ctx", [(a * 4 + b, a * 4 + (b + step) % 4) for a in range(2) for b in range(4)])


def other_core(value):
    return lax.ppermute(value, "dp", [(i, i ^ 1) for i in range(16)])


def spot_of(place, far, step):
    half, row = place // 4, place % 4
    half = 1 - half if far else half
    return half * 4 + (row + step) % 4


def pack_kernel(place, qkv, out, up, down, vec, marks, near, far, qkv_s, out_s, up_s, down_s, vec_s, marks_s, semaphores):
    move = Mover(semaphores)
    arriving = [move.start(*p) for p in ((vec, vec_s), (marks, marks_s), (qkv, qkv_s), (out, out_s), (up, up_s), (down, down_s))]
    for copy in arriving:
        copy.wait()
    vec_row = jnp.concatenate([vec_s[...], jnp.zeros((1, EXTRA - 104), full)], axis=1)
    extra = jnp.concatenate([vec_row, marks_s[...].astype(full), jnp.zeros((6, EXTRA), full)], axis=0).astype(low)
    for is_far, parcel in ((1, far), (0, near)):
        for step in range(4):
            c = spot_of(place[0], is_far, step)
            cut = qkv_s[:, pl.ds(pl.multiple_of(c * QKV, 128), QKV)].astype(low)
            parts = [cut[:, (h * 3 + p) * HD : (h * 3 + p + 1) * HD] for p in range(3) for h in range(HEADS)]
            parcel[step, :, AT_QKV:AT_OUT] = jnp.concatenate(parts, axis=1)
            parcel[step, :, AT_UP : AT_UP + UP] = up_s[:, pl.ds(pl.multiple_of(c * UP, 128), UP)].astype(low)
            parcel[step, :, AT_OUT : AT_OUT + OUT] = out_s[:, pl.ds(pl.multiple_of(c * OUT, 128), OUT)].astype(low)
            parcel[step, :, AT_DOWN : AT_DOWN + UP] = down_s[:, pl.ds(pl.multiple_of(c * UP, 128), UP)].astype(low)
            parcel[step, :, AT_EXTRA:PARCEL] = extra


def regroup_kernel(near, far, *refs):
    for step in range(4):
        refs[step][0] = near[step]
        refs[step][1] = far[step]


def assemble_kernel(place, *refs):
    pieces, whole = refs[:4], refs[4]
    for step in range(4):
        for far in range(2):
            whole[pl.ds(spot_of(place[0], far, step), 1)] = pieces[step][far : far + 1]


def starts_kernel(marks, table, staged, semaphores):
    move = Mover(semaphores)
    whole = marks[...]
    start = jnp.zeros_like(whole)
    for k in range(1, 8):
        start = jnp.where(whole == k, jnp.sum((whole < k).astype(full), keepdims=True), start)
    row = lax.broadcasted_iota(jnp.int32, whole.shape, 0) * ROWS + lax.broadcasted_iota(jnp.int32, whole.shape, 1)
    positions = row.astype(full) - start
    slow = lax.broadcasted_iota(jnp.int32, (ROT // 2, 1), 0)
    frequency = jnp.zeros((ROT // 2, 1), full)
    for i, value in enumerate(FREQUENCIES):
        frequency = jnp.where(slow == i, value, frequency)
    turned = start.T
    for block in range(TP):
        rows = slice(block * ROWS, (block + 1) * ROWS)
        angles = positions[block : block + 1, :] * frequency
        cos_one = jnp.cos(angles).T
        sin_one = jnp.sin(angles).T
        start_one = jnp.broadcast_to(turned[:, block : block + 1], (ROWS, WIDTH - 2 * ROT))
        staged[rows, :] = jnp.concatenate([cos_one, cos_one, sin_one, sin_one, start_one], axis=1)
    move.send(staged, table)
    move.finish()


def norm_kernel(place, *refs):
    pieces, (whole, stored, staged, semaphores) = refs[:4], refs[4:]
    move = Mover(semaphores)
    arriving = [move.start(pieces[step], staged.at[step]) for step in range(4)]
    for step in range(4):
        arriving[step].wait()
        for far in range(2):
            spot = pl.multiple_of(spot_of(place[0], far, step) * ROWS, ROWS)
            normed, _ = normalise(staged[step, far * ROWS : (far + 1) * ROWS, :].astype(full))
            whole[pl.ds(spot, ROWS), :] = normed.astype(low)
    move.send(whole, stored)
    move.finish()


def angles_of(table):
    lane = lax.broadcasted_iota(jnp.int32, table.shape, 1)
    sine = pltpu.roll(table, WIDTH - ROT, 1)
    return tuple(jnp.where(lane < HD, t, pltpu.roll(t, HD, 1)) for t in (table, sine))


def turn(values, cosine, sine):
    lane = lax.broadcasted_iota(jnp.int32, values.shape, 1) % HD
    ahead = pltpu.roll(values, values.shape[1] - ROT // 2, 1)
    behind = pltpu.roll(values, ROT // 2, 1)
    turned = jnp.where(lane < ROT // 2, -ahead, behind)
    return jnp.where(lane < ROT, values * cosine + turned * sine, values)


def masked_scores(q, k, starts, block):
    before = block * BLOCK
    first = starts.astype(jnp.int32)
    key = lax.broadcasted_iota(jnp.int32, (BLOCK, BLOCK), 1)
    row = lax.broadcasted_iota(jnp.int32, (BLOCK, BLOCK), 0)
    near = jnp.where((key <= row) & (key + before >= first), dot(q, k[before:], NT), -1e30)
    if block == 0:
        return near
    key = lax.broadcasted_iota(jnp.int32, (BLOCK, before), 1)
    return jnp.concatenate([jnp.where(key >= first, dot(q, k[:before], NT), -1e30), near], axis=1)


def split_cores(core, rows):
    blocks = rows.reshape(rows.shape[0] // 128, 2, 64, rows.shape[1])
    mine = jnp.where(core == 0, blocks[:, 0], blocks[:, 1])
    others = jnp.where(core == 0, blocks[:, 1], blocks[:, 0])
    return mine.astype(low), others.astype(low)


def forward_kernel(
    place, normed, weights, table,
    attended_out, active_out, slope_out, scaled_out, qkv_out, table_out, bias_out, r0, r1, r2, r3,
    w_s, table_s, scaled, qkv, part_s, attended, active, slope, extra, flat, bias_s, semaphores,
):
    move = Mover(semaphores)
    step_rows = 256
    extra_arrives = move.start(weights.at[:, pl.ds(AT_EXTRA, EXTRA)], extra)
    table_arrives = move.start(table, table_s)
    arriving = [
        move.start(weights.at[pl.ds(r, step_rows), pl.ds(0, MIXED)], w_s.at[pl.ds(r, step_rows), pl.ds(0, MIXED)])
        for r in range(0, D, step_rows)
    ]
    extra_arrives.wait()
    owners = extra[...].astype(full).reshape(128, 8, EXTRA)[:, 0, :]
    for i in range(128):
        flat[:, i * 104 : (i + 1) * 104] = owners[i : i + 1, 0:104]
    bias_s[...] = flat[:, 7 * D : 8 * D] + flat[:, 12 * D : 13 * D]
    move.send(bias_s, bias_out)
    bias_up = flat[:, pl.ds(pl.multiple_of(8 * D + place[0] * UP, UP), UP)]
    bias_qkv = flat[:, pl.ds(pl.multiple_of(4 * D + place[0] * QKV, 128), QKV)]
    bias_qkv = [bias_qkv[:, (h * 3 + p) * HD : (h * 3 + p + 1) * HD] for p in range(3) for h in range(HEADS)]
    base = jnp.concatenate([bias_up] + bias_qkv, axis=1)
    table_arrives.wait()
    for r in range(0, D, 128):
        norms = [flat[:, n * D + r : n * D + r + 128] for n in range(4)]
        norms = jnp.concatenate(norms + [jnp.zeros((4, 128), full)], axis=0).T
        table_s[r : r + 128, AT_NORMS : AT_NORMS + 8] = norms
    for r in range(0, D, 128):
        if r % step_rows == 0:
            arriving[r // step_rows].wait()
        if r == D // 2:
            rest_arrives = move.start(weights.at[:, pl.ds(MIXED, OUT + UP)], w_s.at[:, pl.ds(MIXED, OUT + UP)])
        rows = pl.ds(r, 128)
        w = w_s[rows, 0:MIXED].astype(full)
        gain_one, shift_one, gain_two, shift_two = (table_s[rows, AT_NORMS + i : AT_NORMS + i + 1] for i in range(4))
        w_up, w_qkv = w[:, :UP], w[:, UP:]
        scaled[rows, :] = jnp.concatenate([gain_two * w_up, gain_one * w_qkv], axis=1).astype(low)
        base += jnp.concatenate(
            [jnp.sum(shift_two * w_up, axis=0, keepdims=True), jnp.sum(shift_one * w_qkv, axis=0, keepdims=True)], axis=1
        )
    move.send(scaled, scaled_out)

    for block in range(SEQ // BLOCK):
        rows = pl.ds(block * BLOCK, BLOCK)
        projected = dot(normed[rows, :], scaled[:, AT_QKV:MIXED]) + base[:, AT_QKV:MIXED]
        cosine, sine = angles_of(table_s[rows, :])
        q = (turn(projected[:, 0:WIDTH], cosine, sine).astype(low) * (HD**-0.5)).astype(low)
        k = turn(projected[:, WIDTH : 2 * WIDTH], cosine, sine).astype(low)
        v = projected[:, 2 * WIDTH : 3 * WIDTH].astype(low)
        qkv[rows, :] = jnp.concatenate([q, k, v], axis=1)
        starts = table_s[rows, AT_START : AT_START + 1]
        keys = (block + 1) * BLOCK
        both = []
        half = UP // 2
        for j in range(2):
            cols = slice(j * half, (j + 1) * half)
            hidden = dot(normed[rows, :], scaled[:, cols]) + base[:, cols]
            gate = 0.5 * (1.0 + lax.erf(hidden * (0.5**0.5)))
            active[rows, cols] = (hidden * gate).astype(low)
            inner = gate + hidden * jnp.exp(-0.5 * hidden * hidden) * (1.0 / math.sqrt(2.0 * math.pi))
            slope[rows, cols] = inner.astype(low)
        for head in range(HEADS):
            at = head * HD
            both.append(masked_scores(qkv[rows, at : at + HD], qkv[0:keys, WIDTH + at : WIDTH + at + HD], starts, block))
        for head in range(HEADS):
            at = head * HD
            v = qkv[0:keys, 2 * WIDTH + at : 2 * WIDTH + at + HD]
            scores = both[head]
            most = jnp.max(scores, axis=-1, keepdims=True)
            expo = jnp.exp(scores - most)
            size = jnp.sum(expo, axis=-1, keepdims=True)
            attended[rows, at : at + HD] = (dot(expo.astype(low), v) * (1.0 / size)).astype(low)
            table_s[rows, AT_SIZE + head : AT_SIZE + head + 1] = most + jnp.log(size)
    move.send(qkv, qkv_out)
    move.send(attended, attended_out)
    move.send(table_s, table_out)
    move.send(active, active_out)
    move.send(slope, slope_out)
    rest_arrives.wait()
    for step, part in enumerate((r0, r1, r2, r3)):
        spots = [pl.ds(pl.multiple_of(spot_of(place[0], far, step) * ROWS, ROWS), ROWS) for far in range(2)]
        left = [jnp.concatenate([attended[spot, :], active[spot, :]], axis=1) for spot in spots]
        part_s[step] = dot(jnp.concatenate(left, axis=0), w_s[:, AT_OUT:AT_EXTRA], NT).astype(low)
        move.send(part_s.at[step], part)
    move.finish()


def backward_kernel(
    spots, upstream_total, attended_far, active_far, slope_far, dy0, dy1, dy2, dy3, normed, weights, table, qkv, scaled,
    keep, send, u0, u1, u2, u3,
    dy, w_s, normed_s, table_s, qkv_s, scaled_s, mixed, do_s, kept_s, sums, dq_s, dk_s, dv_s, keep_s, send_s, part_s, early,
    attended, active, slope, semaphores,
):
    move = Mover(semaphores)
    down_arrives = move.start(weights.at[:, pl.ds(AT_OUT, OUT + UP)], w_s.at[:, pl.ds(AT_OUT, OUT + UP)])
    dy_arrive = []

    def dy_start(step, piece):
        for far in range(2):
            spot = pl.multiple_of(spot_of(spots[0], far, step) * ROWS, ROWS)
            dy_arrive.append(move.start(piece.at[pl.ds(far * ROWS, ROWS)], dy.at[pl.ds(spot, ROWS)]))

    dy_start(0, dy0)
    held_arrive = [move.start(*p) for p in ((slope_far, slope), (attended_far, attended))]
    half = UP // 2
    dk_s[...] = jnp.zeros_like(dk_s)
    dv_s[...] = jnp.zeros_like(dv_s)
    early[...] = jnp.zeros_like(early)
    down_arrives.wait()
    for copy in held_arrive:
        copy.wait()
    for step, piece in ((1, dy1), (2, dy2), (3, dy3)):
        dy_start(step, piece)
    table_arrives = move.start(table, table_s)
    qkv_arrives = move.start(qkv, qkv_s)
    scaled_arrives = move.start(scaled, scaled_s)
    totals = [jnp.zeros((1, half), full)] * 2
    later = []
    for step in range(4):
        for copy in dy_arrive[2 * step : 2 * step + 2]:
            copy.wait()
        at = [pl.ds(pl.multiple_of(spot_of(spots[0], far, step) * ROWS, ROWS), ROWS) for far in range(2)]
        dy_now = jnp.concatenate([dy[rows, :] for rows in at], axis=0)
        for j in range(2):
            cols = slice(j * half, (j + 1) * half)
            d_active = dot(dy_now, w_s[:, AT_DOWN + j * half : AT_DOWN + (j + 1) * half])
            d_low = (d_active * jnp.concatenate([slope[rows, cols] for rows in at], axis=0).astype(full)).astype(low)
            for far in range(2):
                mixed[at[far], cols] = d_low[far * ROWS : (far + 1) * ROWS]
            totals[j] += jnp.sum(d_low.astype(full), axis=0, keepdims=True)
        d_out = dot(dy_now, w_s[:, AT_OUT : AT_OUT + OUT]).astype(low)
        for far in range(2):
            d_now = d_out[far * ROWS : (far + 1) * ROWS]
            do_s[at[far], :] = d_now
            product = d_now.astype(full) * attended[at[far], :].astype(full)
            for h in range(HEADS):
                kept_s[at[far], h : h + 1] = jnp.sum(product[:, h * HD : (h + 1) * HD], axis=-1, keepdims=True)
        if step == 0:
            later = [
                move.start(*p)
                for p in (
                    (normed, normed_s), (active_far, active),
                    (weights.at[:, pl.ds(0, MIXED)], w_s.at[:, pl.ds(0, MIXED)]),
                )
            ]
    hidden_total = jnp.concatenate(totals, axis=1)

    table_arrives.wait()
    qkv_arrives.wait()
    for copy in later:
        copy.wait()
    lane = lax.broadcasted_iota(jnp.int32, (BLOCK, 128), 1)
    for block in range(SEQ // BLOCK):
        rows = pl.ds(block * BLOCK, BLOCK)
        starts = table_s[rows, AT_START : AT_START + 1]
        keys = (block + 1) * BLOCK
        places = pl.ds(block * (BLOCK // 128), BLOCK // 128)
        gain_two, shift_two = (table_s[rows, AT_NORMS + n : AT_NORMS + n + 1] for n in (2, 3))
        core_up = dot(normed_s[:, rows], mixed[:, 0:UP], TN)
        w_up = w_s[rows, 0:UP].astype(full)
        found = [jnp.sum(t, axis=1, keepdims=True) for t in (w_up * core_up, w_up * hidden_total)]
        sums[rows, :] = jnp.where(lane == 2, found[0], found[1])
        grad_up = gain_two * core_up + shift_two * hidden_total
        grad_down = dot(dy[:, rows], active[...], TN)
        grad_out = dot(dy[:, rows], attended[...], TN)
        mine, others = split_cores(spots[1], jnp.concatenate([grad_up, grad_down, grad_out], axis=1))
        keep_s[places, :, 0:FEED] = mine
        send_s[places, :, 0:FEED] = others
        for head in range(HEADS):
            at = head * HD
            lanes = pl.ds(at, HD)
            q = qkv_s[rows, at : at + HD]
            k = qkv_s[0:keys, WIDTH + at : WIDTH + at + HD]
            v = qkv_s[0:keys, 2 * WIDTH + at : 2 * WIDTH + at + HD]
            d_o = do_s[rows, lanes]
            scores = masked_scores(q, k, starts, block)
            weight = jnp.exp(scores - table_s[rows, AT_SIZE + head : AT_SIZE + head + 1])
            d_weight = dot(d_o, v, NT)
            d_scores = (weight * (d_weight - kept_s[rows, head : head + 1])).astype(low)
            dq_s[rows, lanes] = dot(d_scores, k) * (HD**-0.5)
            dk_s[0:keys, lanes] += dot(d_scores, q, TN)
            dv_s[0:keys, lanes] += dot(weight.astype(low), d_o, TN)
    total = jnp.zeros((1, QKV), full)
    for block in range(SEQ // BLOCK):
        rows = pl.ds(block * BLOCK, BLOCK)
        cosine, sine = angles_of(table_s[rows, :])
        sine = -sine
        back_low = jnp.concatenate(
            [turn(dq_s[rows, :], cosine, sine), turn(dk_s[rows, :], cosine, sine), dv_s[rows, :]], axis=1
        ).astype(low)
        mixed[rows, AT_QKV:MIXED] = back_low
        total += jnp.sum(back_low.astype(full), axis=0, keepdims=True)

    scaled_arrives.wait()
    for step, part in ((1, u1), (2, u2), (3, u3), (0, u0)):
        left = [mixed[pl.ds(pl.multiple_of(spot_of(spots[0], far, step) * ROWS, ROWS), ROWS), :] for far in range(2)]
        part_s[step] = dot(jnp.concatenate(left, axis=0), scaled_s[...], NT).astype(low)
        move.send(part_s.at[step], part)

    for i in range(D // BLOCK):
        rows = pl.ds(i * BLOCK, BLOCK)
        places = pl.ds(i * (BLOCK // 128), BLOCK // 128)
        gain_one, shift_one = (table_s[rows, AT_NORMS + n : AT_NORMS + n + 1] for n in (0, 1))
        core_qkv = dot(normed_s[:, rows], mixed[:, UP:MIXED], TN)
        w_qkv = w_s[rows, UP:MIXED].astype(full)
        found = [jnp.sum(t, axis=1, keepdims=True) for t in (w_qkv * core_qkv, w_qkv * total)]
        sums[rows, :] = jnp.where(lane == 0, found[0], jnp.where(lane == 1, found[1], sums[rows, :]))
        mine, others = split_cores(spots[1], gain_one * core_qkv + shift_one * total)
        keep_s[places, :, FEED : FEED + QKV] = mine
        send_s[places, :, FEED : FEED + QKV] = others
        for staged, target in ((send_s, send), (keep_s, keep)):
            done = (places, slice(None), pl.ds(0, FEED + QKV))
            move.send(staged.at[done], target.at[done])
    for r in range(0, D, 128):
        turned = sums[r : r + 128, :].T
        for n in range(4):
            early[:, n * D + r : n * D + r + 128] = turned[n : n + 1, :]
    bias_total = jnp.concatenate(
        [total[:, part * WIDTH + h * HD : part * WIDTH + (h + 1) * HD] for h in range(HEADS) for part in range(3)], axis=1
    )
    early[:, pl.ds(pl.multiple_of(4 * D + spots[0] * QKV, 128), QKV)] = bias_total
    early[:, 7 * D : 8 * D] = upstream_total[...]
    early[:, pl.ds(pl.multiple_of(8 * D + spots[0] * UP, UP), UP)] = hidden_total
    early[:, 12 * D : 13 * D] = upstream_total[...]
    for zl in range(8):
        parts = []
        for core in range(2):
            lines = []
            for c in range(TP):
                at = ((zl * 2 + core) * TP + c) * 104
                lines.append(jnp.concatenate([early[:, at : at + 104], jnp.zeros((1, EXTRA - 104), full)], axis=1))
                lines.append(jnp.zeros((7, EXTRA), full))
            parts.append(jnp.concatenate(lines, axis=0))
        keep_s[zl, :, FEED + QKV : PARCEL] = jnp.where(spots[1] == 0, parts[0], parts[1]).astype(low)
        send_s[zl, :, FEED + QKV : PARCEL] = jnp.where(spots[1] == 0, parts[1], parts[0]).astype(low)
    for staged, target in ((send_s, send), (keep_s, keep)):
        done = (slice(None), slice(None), pl.ds(FEED + QKV, EXTRA))
        move.send(staged.at[done], target.at[done])
    move.finish()


def update_kernel(grads, *refs):
    state, new = refs[:15], refs[15:30]

    def update(index, columns, gradient, rate, decay):
        results = adamw(*(state[3 * index + i][:, columns] for i in range(3)), gradient.astype(full), rate, decay)
        for i in range(3):
            new[3 * index + i][:, columns] = results[i]

    total = jnp.zeros((1, 104), full)
    for c in range(TP):
        at = FEED
        parts = [[grads[c, :, at + (p * HEADS + h) * HD : at + (p * HEADS + h + 1) * HD] for p in range(3)] for h in range(HEADS)]
        qkv = jnp.concatenate([part for head in parts for part in head], axis=1)
        update(0, slice(c * QKV, (c + 1) * QKV), qkv, 2.0 / math.sqrt(D), 0.1)
        update(1, slice(c * OUT, (c + 1) * OUT), grads[c, :, 2 * UP : FEED], 8.0 / math.sqrt(D), 0.1)
        update(2, slice(c * UP, (c + 1) * UP), grads[c, :, 0:UP], 2.0 / math.sqrt(D), 0.1)
        update(3, slice(c * UP, (c + 1) * UP), grads[c, :, UP : 2 * UP], 2.0 / math.sqrt(FF), 0.1)
        total += grads[c, :, FEED + QKV : FEED + QKV + 104].astype(full)[0:1, :]
    update(4, slice(0, 104), total, 0.5, 0.0)


def shift_rows(parts):
    return (parts[0], along(parts[1], 1), along(parts[2], 2), along(parts[3], -1))


def sum_rows(parts):
    near = sum(part[:ROWS].astype(full) for part in parts)
    far = sum(part[ROWS:].astype(full) for part in parts)
    return near, far.astype(low)


def local(
    inputs, segments, cotangent, qkv_weight, out_weight, up_weight, down_weight, vectors,
    qkv_first, qkv_second, out_first, out_second, up_first, up_second, down_first, down_second, vec_first, vec_second,
):
    place = lax.axis_index("ctx")
    rank = lax.axis_index("dp")
    place_one = place.reshape(1).astype(jnp.int32)
    core = lax.rem(rank, 2)
    spots = jnp.stack([place, core]).astype(jnp.int32)
    tokens = inputs[0]
    upstream = cotangent[0]

    quarter, piece = ((4, 8, PARCEL), low), ((2, 8, PARCEL), low)
    near, far = call(
        pack_kernel, "pack", [(quarter, VMEM)] * 2,
        [(place_one, SMEM)] + [(o, FAR) for o in (qkv_weight, out_weight, up_weight, down_weight, vectors.reshape(1, 104), segments)],
        scratch=[((8, n), full) for n in (3 * D, D, FF, FF)] + [((1, 104), full), ((1, ROWS), jnp.int32)], copies=6,
    )
    far, later_tokens = lax.optimization_barrier((across(far), tokens))
    far_tokens = across(later_tokens)
    sends = call(regroup_kernel, "regroup", [(piece, VMEM)] * 4, [(near, VMEM), (far, VMEM)])
    pieces = (sends[0], along(sends[3], -1), along(sends[2], 2), along(sends[1], 1))
    pieces, far_tokens = lax.optimization_barrier((pieces, far_tokens))
    (parcel,) = call(
        assemble_kernel, "assemble", [(((TP, 8, PARCEL), low), VMEM)], [(place_one, SMEM)] + [(o, VMEM) for o in pieces]
    )

    def rows_of(value, far_value):
        pair = jnp.concatenate([value, far_value], axis=0)
        return (pair, along(pair, -1), along(pair, 2), along(pair, 1))

    x_pieces = rows_of(tokens, far_tokens)
    far_upstream = across(upstream)
    marks = parcel[:, 1, AT_EXTRA:PARCEL].astype(full)
    (table,) = call(
        starts_kernel, "starts", [(((SEQ, WIDTH), full), FAR)], [(marks, VMEM)], scratch=[((SEQ, WIDTH), full)], copies=1
    )
    x_pieces, upstream, far_upstream, table = lax.optimization_barrier((x_pieces, upstream, far_upstream, table))
    dy_pieces = rows_of(upstream, far_upstream)
    weights = lax.all_gather(parcel.reshape(64, PARCEL), "dp", axis=0, tiled=True)

    square = ((SEQ, D), low)
    normed, normed_far = call(
        norm_kernel, "norm", [(square, VMEM), (square, FAR)], [(place_one, SMEM)] + [(o, FAR) for o in x_pieces],
        scratch=[((4, 2 * ROWS, D), low)], copies=5,
    )
    weights, normed, table = lax.optimization_barrier((weights, normed, table))
    pairs = ((2 * ROWS, D), low)
    head_rows, table_type, scaled_type, qkv_type, hidden_type = ((SEQ, WIDTH), low), ((SEQ, WIDTH), full), ((D, MIXED), low), ((SEQ, QKV), low), ((SEQ, UP), low)
    attended, active, slope, scaled, qkv, table, bias_out, *r_parts = call(
        forward_kernel, "forward",
        [(o, FAR) for o in (head_rows, hidden_type, hidden_type, scaled_type, qkv_type, table_type, ((1, D), full))] + [(pairs, FAR)] * 4,
        [(place_one, SMEM), (normed, VMEM), (weights, FAR), (table, FAR)],
        scratch=[
            ((D, AT_EXTRA), low), table_type, scaled_type, qkv_type, ((4, 2 * ROWS, D), low), head_rows, hidden_type, hidden_type,
            ((D, EXTRA), low), ((1, 13 * D), full), ((1, D), full),
        ],
        copies=18,
    )
    r_parts = shift_rows(r_parts)

    attended, dy_pieces = lax.optimization_barrier((attended, dy_pieces))
    upstream_total = jnp.sum(upstream.astype(full), axis=0, keepdims=True)
    parcel_type, kept_type = ((8, 64, PARCEL), low), ((SEQ, WIDTH), full)
    keep, send, *u_parts = call(
        backward_kernel, "backward",
        [(parcel_type, FAR)] * 2 + [(pairs, FAR)] * 4,
        [(spots, SMEM), (upstream_total, VMEM)]
        + [(o, FAR) for o in (attended, active, slope) + dy_pieces + (normed_far, weights, table, qkv, scaled)],
        scratch=[
            square, ((D, AT_EXTRA), low), square, table_type, qkv_type, scaled_type,
            ((SEQ, MIXED), low), head_rows, kept_type, kept_type, kept_type, kept_type, kept_type,
            parcel_type, parcel_type, ((4, 2 * ROWS, D), low), ((1, 13 * D), full),
            head_rows, hidden_type, hidden_type,
        ],
        copies=32,
    )
    keep, send, r_parts = lax.optimization_barrier((keep, send, r_parts))
    u_parts = shift_rows(u_parts)
    grads = (keep.astype(full) + other_core(send).astype(full)).astype(low)
    result, result_far = sum_rows(r_parts)
    grads, result_far = lax.optimization_barrier((grads, result_far))
    lanes = [[(zl * 2 + k) for zl in range(8)] for k in range(2)]
    grads = lax.all_to_all(grads, "dp", 0, 0, axis_index_groups=lanes, tiled=True)
    d_own, d_far = sum_rows(u_parts)
    grads, d_far, result_far = lax.optimization_barrier((grads, d_far, across(result_far)))
    grads = jnp.sum(grads.astype(full), axis=0).astype(low).reshape(TP, 8, PARCEL)
    own_grads = lax.all_to_all(grads, "ctx", 0, 0, tiled=True)
    d_own = d_own + across(d_far).astype(full)
    result = result + result_far.astype(full)

    outputs = tokens.astype(full) + result + bias_out
    own, rate = normalise(tokens.astype(full))
    d_tokens = rate * (
        d_own - jnp.mean(d_own, axis=-1, keepdims=True) - own * jnp.mean(d_own * own, axis=-1, keepdims=True)
    )
    input_grad = upstream.astype(full) + d_tokens

    outputs, input_grad, own_grads = lax.optimization_barrier((outputs.astype(low), input_grad, own_grads))
    state = (
        (qkv_weight, qkv_first, qkv_second), (out_weight, out_first, out_second), (up_weight, up_first, up_second),
        (down_weight, down_first, down_second), tuple(v.reshape(1, 104) for v in (vectors, vec_first, vec_second)),
    )
    state = [array for triple in state for array in triple]
    new = call(
        update_kernel, "update", [((o.shape, full), NEAR) for o in state], [(own_grads, VMEM)] + [(o, VMEM) for o in state],
    )
    return (outputs[None], input_grad[None]) + tuple(new[:12]) + tuple(v.reshape(104) for v in new[12:])


def solution(mesh):
    tokens = P("dp", "ctx", None)
    matrix = P(("dp", "ctx"), None)
    vector = P(("dp", "ctx"))
    return jax.shard_map(
        local,
        mesh=mesh,
        in_specs=(tokens, P("dp", "ctx"), tokens) + (matrix,) * 4 + (vector,) + (matrix,) * 8 + (vector,) * 2,
        out_specs=(tokens, tokens) + (matrix,) * 12 + (vector,) * 3,
        check_vma=False,
    )
```
